32 devices in a mesh: seq: 8 (over y, x, core), pipe: 4 (over z).
Axes of the slice: x: 2, y: 2, z: 4, core: 2. Of those that a mesh axis runs over, the one named last changes fastest.
Arguments:
- section_inputs: bfloat16 [4, 1024, 1536], P('pipe', 'seq'), may hold values from -6 to 6
- cotangent: bfloat16 [1024, 1536], P('seq'), may hold values from -6 to 6
- gain: float32 [4, 1536], P('pipe'), may hold values from 0.25 to 1.75
- w_gate: bfloat16 [4, 1536, 1536], P('pipe'), may hold values from -0.15625 to 0.15625
- w_out: bfloat16 [4, 1536, 1536], P('pipe'), may hold values from -0.15625 to 0.15625
- mix_first: bfloat16 [4, 16, 64, 64], P('pipe', 'seq'), may hold values from -0.75 to 0.75
- mix_second: bfloat16 [4, 16, 64, 64], P('pipe', 'seq'), may hold values from -0.75 to 0.75
Outputs:
- grad_inputs: bfloat16 [4, 1024, 1536], P('pipe', 'seq')
- grad_first: float32 [4, 16, 64, 64], P('pipe', 'seq')
- grad_second: float32 [4, 16, 64, 64], P('pipe', 'seq')
The draws below stay inside these ranges and needn't reach their ends.
All inputs are finite; a program needn't handle non-finite values.
Results may differ from the reference program's by a relative error of at most 0.025.
Values may be sent and summed in bfloat16 or wider, within the bound.
No kernel may reach another device: no remote copies, remote signals or barrier semaphores. Data moves between devices by JAX's collectives and lax.ppermute only.
A program may use at most 64 MiB of HBM per device.

```python
import jax
import jax.numpy as jnp
from jax import lax

D = 1536
BLOCK = 64
LAYERS = 4
TOKENS = 1024
BLOCKS = 16
N_PIPE = 4


def block_scale(stream_key, extent, cuts, low, top_value):
    def one(position, shards_of):
        steps = jax.random.uniform(jax.random.fold_in(jax.random.fold_in(stream_key, 6), position), (shards_of,), jnp.float32, low / len(cuts), top_value / len(cuts))
        return jnp.repeat(jnp.exp(steps), extent[position] // shards_of).reshape((-1,) + (1,) * (len(extent) - position - 1))

    factor_of = one(*cuts[0])
    for cut in cuts[1:]:
        factor_of = factor_of * one(*cut)
    return factor_of


def normal_values(stream_key, shape, width, bound, pieces=(), dtype=jnp.bfloat16):
    level = block_scale(stream_key, shape, pieces, -0.22, 0.18) if pieces else 1.0
    result = jax.random.normal(stream_key, shape, jnp.float32) * width * level
    return jnp.minimum(jnp.maximum(result, -bound), bound).astype(dtype)


def setup_inputs(seed: int = 0) -> dict:
    key_of = jax.random.split(jax.random.key(seed), 8)
    section_inputs = normal_values(key_of[0], (LAYERS, TOKENS, D), 1.0, 6.0, ((0, 4), (1, 8)))
    cotangent = normal_values(key_of[1], (TOKENS, D), 1.0, 6.0, ((0, 8),))
    gain = jnp.clip(1.0 + 0.15 * jax.random.normal(key_of[2], (LAYERS, D), jnp.float32), 0.25, 1.75)
    w_gate = normal_values(key_of[3], (LAYERS, D, D), D ** -0.5, 0.15625, ((0, 4),))
    w_out = normal_values(key_of[4], (LAYERS, D, D), D ** -0.5, 0.15625, ((0, 4),))
    mix_first = normal_values(key_of[5], (LAYERS, BLOCKS, BLOCK, BLOCK), BLOCK ** -0.5, 0.75, ((0, 4), (1, 8)))
    mix_second = normal_values(key_of[6], (LAYERS, BLOCKS, BLOCK, BLOCK), BLOCK ** -0.5, 0.75, ((0, 4), (1, 8)))
    return {"section_inputs": section_inputs, "cotangent": cotangent, "gain": gain, "w_gate": w_gate, "w_out": w_out, "mix_first": mix_first, "mix_second": mix_second}


def layer_grad(inputs, incoming, gain_row, weight_gate, weight_out, first_blocks, second_blocks):
    features = inputs.astype(jnp.float32)
    inv_rms = lax.rsqrt(lax.optimization_barrier(jnp.mean(features * features, axis=-1, keepdims=True)) + 1e-06)
    unit_rows = features * inv_rms
    normed = (unit_rows * gain_row).astype(jnp.bfloat16)
    normed_blocks = normed.reshape(BLOCKS, BLOCK, D)
    first_out = jnp.einsum('kij,kjc->kic', first_blocks.astype(jnp.float32), normed_blocks.astype(jnp.float32)).astype(jnp.bfloat16)
    moved_blocks = jnp.transpose(first_out, (1, 0, 2)).reshape(BLOCKS, BLOCK, D)
    mixer_out = jnp.einsum('kij,kjc->kic', second_blocks.astype(jnp.float32), moved_blocks.astype(jnp.float32)).reshape(TOKENS, D)
    gate_pre = jnp.dot(normed, weight_gate, preferred_element_type=jnp.float32)
    sigma = jax.nn.sigmoid(gate_pre)
    delta_hidden = jnp.dot(incoming, weight_out.T, preferred_element_type=jnp.float32)
    delta_mix = (delta_hidden * gate_pre * sigma).astype(jnp.bfloat16)
    delta_gate = (delta_hidden * mixer_out * sigma * (1.0 + gate_pre * (1.0 - sigma))).astype(jnp.bfloat16)
    mix_blocks = delta_mix.reshape(BLOCKS, BLOCK, D)
    delta_moved = jnp.einsum('kij,kic->kjc', second_blocks.astype(jnp.float32), mix_blocks.astype(jnp.float32)).astype(jnp.bfloat16)
    delta_mid = jnp.transpose(delta_moved.reshape(BLOCK, BLOCKS, D), (1, 0, 2))
    first_back = jnp.einsum('kij,kic->kjc', first_blocks.astype(jnp.float32), delta_mid.astype(jnp.float32)).reshape(TOKENS, D)
    gate_back = jnp.dot(delta_gate, weight_gate.T, preferred_element_type=jnp.float32)
    delta_norm = (first_back + gate_back) * gain_row
    centred = delta_norm - unit_rows * lax.optimization_barrier(jnp.mean(delta_norm * unit_rows, axis=-1, keepdims=True))
    outgoing = (incoming.astype(jnp.float32) + inv_rms * centred).astype(jnp.bfloat16)
    grad_first_layer = jnp.einsum('kic,kjc->kij', delta_mid.astype(jnp.float32), normed_blocks.astype(jnp.float32))
    grad_second_layer = jnp.einsum('kic,kjc->kij', mix_blocks.astype(jnp.float32), moved_blocks.astype(jnp.float32))
    return (outgoing, grad_first_layer, grad_second_layer)

def reference(section_inputs, cotangent, gain, w_gate, w_out, mix_first, mix_second):
    incoming = cotangent
    input_grads = []
    first_grads = []
    second_grads = []
    for layer_index in reversed(range(N_PIPE)):
        outgoing, grad_first_layer, grad_second_layer = layer_grad(section_inputs[layer_index], incoming, gain[layer_index], w_gate[layer_index], w_out[layer_index], mix_first[layer_index], mix_second[layer_index])
        input_grads.insert(0, outgoing)
        first_grads.insert(0, grad_first_layer)
        second_grads.insert(0, grad_second_layer)
        incoming = outgoing
    return (jnp.stack(input_grads), jnp.stack(first_grads), jnp.stack(second_grads))
```

```python
import jax
import jax.numpy as jnp
from jax import lax
from jax.sharding import PartitionSpec as P

ROWS_BY_ROWS = (((1,), (1,)), ((), ()))


def dot(left, right):
    return jnp.dot(left, right, preferred_element_type=jnp.float32)


def dot_rows(left, right):
    return lax.dot_general(left, right, ROWS_BY_ROWS, preferred_element_type=jnp.float32)


def swap(block, offset):
    count = lax.axis_size("seq")
    return lax.ppermute(block, "seq", [(i, i ^ offset) for i in range(count)])


def exchange(send, count):
    half = send.shape[0] // 2
    piece = half // (count // 2)
    kept = send[:half]
    got = swap(send[half:], 1)
    parts = [kept[:piece], got[:piece]]
    for chip in range(1, count // 2):
        rows = slice(chip * piece, (chip + 1) * piece)
        parts.append(swap(jnp.concatenate([kept[rows], got[rows]]), 2 * chip))
    return jnp.concatenate(parts)


def block_diagonal(blocks):
    count, rows, columns = blocks.shape
    zero = jnp.zeros((rows, columns), blocks.dtype)
    return jnp.concatenate(
        [
            jnp.concatenate([blocks[k] if k == j else zero for j in range(count)], axis=1)
            for k in range(count)
        ],
        axis=0,
    )


def diagonal_blocks(matrix, count):
    rows, columns = matrix.shape[0] // count, matrix.shape[1] // count
    return jnp.stack(
        [
            matrix[k * rows : (k + 1) * rows, k * columns : (k + 1) * columns]
            for k in range(count)
        ]
    )


def per_device(section_inputs, cotangent, gain, w_gate, w_out, mix_first, mix_second):
    inputs = section_inputs[0]
    gain_row = gain[0]
    weight_gate = w_gate[0]
    weight_out = w_out[0]
    row_count, _ = inputs.shape
    local_blocks, block_rows = mix_first.shape[1:3]
    seq_count = lax.axis_size("seq")
    section_count = lax.axis_size("pipe")
    section_index = lax.axis_index("pipe")
    me = lax.axis_index("seq")
    steps = block_rows // seq_count

    position = jnp.arange(row_count)
    partner_send = position // (row_count // 2) + 2 * (
        position // (local_blocks * steps) % (seq_count // 2)
    )
    partner_recv = position // (local_blocks * steps)
    block = position // steps % local_blocks
    step = position % steps

    def first_rows(partner):
        return block * block_rows + (me ^ partner) * steps + step

    def second_rows(partner):
        return step * (seq_count * local_blocks) + (me ^ partner) * local_blocks + block

    def one_hot(rows):
        return (rows[:, None] == position[None, :]).astype(jnp.bfloat16)

    def permuted(rows, matrix):
        return dot(one_hot(rows), matrix).astype(jnp.bfloat16)

    first_full = block_diagonal(mix_first[0])
    second_full = block_diagonal(mix_second[0])
    first_send = permuted(first_rows(partner_send), first_full)
    first_recv = permuted(first_rows(partner_recv), first_full)
    second_send = permuted(second_rows(partner_send), second_full.T)
    second_recv = permuted(second_rows(partner_recv), second_full.T)

    features = inputs.astype(jnp.float32)
    inv_rms = lax.rsqrt(jnp.mean(features * features, axis=-1, keepdims=True) + 1e-06)
    unit_rows = features * inv_rms
    normed = (unit_rows * gain_row).astype(jnp.bfloat16)
    moved = exchange(dot(first_send, normed).astype(jnp.bfloat16), seq_count)
    gate_pre = dot(normed, weight_gate)
    sigma = jax.nn.sigmoid(gate_pre)
    mix_factor = gate_pre * sigma
    mixer_out = dot(second_recv.T, moved)
    gate_factor = mixer_out * sigma * (1.0 + gate_pre * (1.0 - sigma))

    incoming = cotangent
    outgoing_kept = jnp.zeros_like(cotangent)
    first_kept = jnp.zeros((row_count, row_count), jnp.float32)
    second_kept = jnp.zeros((row_count, row_count), jnp.float32)
    for tick_index in range(section_count):
        sender = section_count - 1 - tick_index
        active = section_index == sender
        delta_hidden = dot_rows(incoming, weight_out)
        delta_mix = (delta_hidden * mix_factor).astype(jnp.bfloat16)
        delta_gate = (delta_hidden * gate_factor).astype(jnp.bfloat16)
        delta_mid = exchange(dot(second_send, delta_mix).astype(jnp.bfloat16), seq_count)
        gate_back = dot_rows(delta_gate, weight_gate)
        first_back = dot(first_recv.T, delta_mid)
        delta_norm = (first_back + gate_back) * gain_row
        centred = delta_norm - unit_rows * jnp.mean(delta_norm * unit_rows, axis=-1, keepdims=True)
        outgoing = (incoming.astype(jnp.float32) + inv_rms * centred).astype(jnp.bfloat16)
        if sender > 0:
            incoming = lax.ppermute(outgoing, "pipe", [(sender, sender - 1)])
        outgoing_kept = jnp.where(active, outgoing, outgoing_kept)
        first_kept = jnp.where(active, dot_rows(delta_mid, normed), first_kept)
        second_kept = jnp.where(active, dot_rows(delta_mix, moved), second_kept)

    def unpermuted(rows, matrix):
        return jnp.dot(
            one_hot(rows).astype(jnp.float32).T,
            matrix,
            precision=lax.Precision.HIGHEST,
            preferred_element_type=jnp.float32,
        )

    grad_first = diagonal_blocks(unpermuted(first_rows(partner_recv), first_kept), local_blocks)
    grad_second = diagonal_blocks(
        unpermuted(second_rows(partner_recv), second_kept.T).T, local_blocks
    )
    return (outgoing_kept[None], grad_first[None], grad_second[None])


def solution(mesh):
    placed = (
        P("pipe", "seq", None),
        P("seq", None),
        P("pipe", None),
        P("pipe", None, None),
        P("pipe", None, None),
        P("pipe", "seq", None, None),
        P("pipe", "seq", None, None),
    )
    return jax.shard_map(
        per_device,
        mesh=mesh,
        in_specs=placed,
        out_specs=(
            P("pipe", "seq", None),
            P("pipe", "seq", None, None),
            P("pipe", "seq", None, None),
        ),
        check_vma=False,
    )
```

```python
import functools

import jax
import jax.numpy as jnp
from jax import lax
from jax.experimental import pallas as pl
from jax.experimental.pallas import tpu as pltpu
from jax.sharding import PartitionSpec as P

ROWS_BY_ROWS = (((1,), (1,)), ((), ()))
WHOLE = pl.BlockSpec(memory_space=pltpu.VMEM)
ANYWHERE = pl.BlockSpec(memory_space=pl.ANY)
SCALAR = pl.BlockSpec(memory_space=pltpu.SMEM)
PARAMS = pltpu.CompilerParams(vmem_limit_bytes=12 << 20)


def dot(left, right):
    return jnp.dot(left, right, preferred_element_type=jnp.float32)


def dot_rows(left, right):
    return lax.dot_general(left, right, ROWS_BY_ROWS, preferred_element_type=jnp.float32)


def swap(block, offset):
    count = lax.axis_size("seq")
    return lax.ppermute(block, "seq", [(i, i ^ offset) for i in range(count)])


def chip_exchange(kept, got, count):
    piece = kept.shape[0] // (count // 2)
    parts = [kept[:piece], got[:piece]]
    for chip in range(1, count // 2):
        rows = slice(chip * piece, (chip + 1) * piece)
        parts.append(swap(jnp.concatenate([kept[rows], got[rows]]), 2 * chip))
    return jnp.concatenate(parts)


def chunks(size, count):
    return [slice(i * size // count, (i + 1) * size // count) for i in range(count)]


def block_diagonal(blocks):
    zero = jnp.zeros(blocks[0].shape, blocks[0].dtype)
    return jnp.concatenate(
        [
            jnp.concatenate([b if k == j else zero for j in range(len(blocks))], axis=1)
            for k, b in enumerate(blocks)
        ],
        axis=0,
    )


def log2(size):
    assert size & (size - 1) == 0
    return size.bit_length() - 1


class Order:
    def __init__(self, row_count, local_blocks, block_rows, seq_count):
        self.row_count = row_count
        self.local_blocks = local_blocks
        self.block_rows = block_rows
        self.seq_count = seq_count
        self.steps = block_rows // seq_count
        self.group = local_blocks * self.steps

    def recv_partner(self, position):
        return position >> log2(self.group)

    def send_partner(self, position):
        chip = (position >> log2(self.group)) & (self.seq_count // 2 - 1)
        return (position >> log2(self.row_count // 2)) + 2 * chip

    def block(self, position):
        return (position >> log2(self.steps)) & (self.local_blocks - 1)

    def first_rows(self, me, partner, position):
        step = position & (self.steps - 1)
        return self.block(position) * self.block_rows + (me ^ partner) * self.steps + step

    def second_rows(self, me, partner, position):
        step = position & (self.steps - 1)
        device = me ^ partner
        return (step * self.seq_count + device) * self.local_blocks + self.block(position)


def prepare_kernel(
    order, me_ref, x_ref, gain_ref, first_ref, second_ref, gate_ref,
    normed_ref, inv_ref, keep_ref, give_ref, first_recv_ref, second_send_ref, second_recv_ref,
    gate_held, sems,
):
    copies = [
        pltpu.make_async_copy(gate_ref.at[rows], gate_held.at[rows], sems.at[i])
        for i, rows in enumerate(chunks(gate_ref.shape[0], sems.shape[0]))
    ]
    for copy in copies:
        copy.start()
    me = me_ref[0]
    square = (order.row_count, order.row_count)
    down = lax.broadcasted_iota(jnp.int32, square, 0)
    across = lax.broadcasted_iota(jnp.int32, square, 1)

    def one_hot(matches):
        return jnp.where(matches, 1.0, 0.0).astype(jnp.bfloat16)

    def rounded(left, right):
        return dot(left, right).astype(jnp.bfloat16)

    first = block_diagonal([first_ref[k].astype(jnp.float32) for k in range(order.local_blocks)])
    second = block_diagonal([second_ref[k].astype(jnp.float32) for k in range(order.local_blocks)])
    sent, received = order.send_partner(down), order.recv_partner(across)
    first_send = rounded(
        one_hot(order.first_rows(me, sent, down) == across), first.astype(jnp.bfloat16)
    )
    second_send_ref[...] = rounded(
        one_hot(order.second_rows(me, sent, down) == across), second.T.astype(jnp.bfloat16)
    )
    first_recv_ref[...] = rounded(
        first.T.astype(jnp.bfloat16), one_hot(order.first_rows(me, received, across) == down)
    )
    second_recv_ref[...] = rounded(
        second.astype(jnp.bfloat16), one_hot(order.second_rows(me, received, across) == down)
    )
    features = x_ref[...].astype(jnp.float32)
    inv_rms = lax.rsqrt(jnp.mean(features * features, axis=-1, keepdims=True) + 1e-06)
    inv_ref[...] = inv_rms
    normed = (features * inv_rms * gain_ref[...]).astype(jnp.bfloat16)
    normed_ref[...] = normed
    send = rounded(first_send, normed)
    half = order.row_count // 2
    keep_ref[...] = send[:half]
    give_ref[...] = send[half:]
    for copy in copies:
        copy.wait()


def begin_kernel(
    normed_ref, gate_ref, incoming_ref, out_ref, second_send_ref,
    mix_factor_ref, slope_ref, hidden_ref, mix_ref, keep_ref, give_ref, out_held, sems,
):
    parts = chunks(out_ref.shape[0], sems.shape[0])
    copies = [
        pltpu.make_async_copy(out_ref.at[rows], out_held.at[rows], sems.at[i])
        for i, rows in enumerate(parts)
    ]
    for copy in copies:
        copy.start()
    half = keep_ref.shape[0]
    for columns in parts:
        gate_pre = dot(normed_ref[...], gate_ref[:, columns])
        sigma = jax.nn.sigmoid(gate_pre)
        mix_factor_ref[:, columns] = gate_pre * sigma
        slope_ref[:, columns] = sigma * (1.0 + gate_pre * (1.0 - sigma))
    for columns, copy in zip(parts, copies):
        copy.wait()
        hidden = dot_rows(incoming_ref[...], out_held[columns])
        hidden_ref[:, columns] = hidden
        mix = (hidden * mix_factor_ref[:, columns]).astype(jnp.bfloat16)
        mix_ref[:, columns] = mix
        send = dot(second_send_ref[...], mix).astype(jnp.bfloat16)
        keep_ref[:, columns] = send[:half]
        give_ref[:, columns] = send[half:]


def transpose_kernel(gate_ref, out_ref, gate_turned_ref, out_turned_ref):
    for rows in chunks(gate_ref.shape[0], 6):
        gate_turned_ref[:, rows] = gate_ref[rows].T
        out_turned_ref[:, rows] = out_ref[rows].T


def prepare(order, me, inputs, gain_row, first_blocks, second_blocks, weight_gate):
    row_count, width = inputs.shape
    square = pltpu.VMEM((row_count, row_count), jnp.bfloat16)
    half = pltpu.VMEM((row_count // 2, width), jnp.bfloat16)
    return pl.pallas_call(
        functools.partial(prepare_kernel, order),
        in_specs=[SCALAR, WHOLE, WHOLE, WHOLE, WHOLE, ANYWHERE],
        out_specs=[WHOLE] * 8,
        out_shape=[
            pltpu.VMEM((row_count, width), jnp.bfloat16),
            pltpu.VMEM((row_count, 1), jnp.float32),
            half,
            half,
            square,
            square,
            square,
            pltpu.VMEM(weight_gate.shape, jnp.bfloat16),
        ],
        scratch_shapes=[pltpu.SemaphoreType.DMA((6,))],
        compiler_params=PARAMS,
        name="prepare",
    )(me, inputs, gain_row, first_blocks, second_blocks, weight_gate)


def begin(normed, gate_held, incoming, weight_out, second_send):
    row_count, width = normed.shape
    half = pltpu.VMEM((row_count // 2, width), jnp.bfloat16)
    full = pltpu.VMEM((row_count, width), jnp.float32)
    return pl.pallas_call(
        begin_kernel,
        in_specs=[WHOLE, WHOLE, WHOLE, ANYWHERE, WHOLE],
        out_specs=[WHOLE] * 7,
        out_shape=[
            full,
            full,
            full,
            pltpu.VMEM((row_count, width), jnp.bfloat16),
            half,
            half,
            pltpu.VMEM(weight_out.shape, jnp.bfloat16),
        ],
        scratch_shapes=[pltpu.SemaphoreType.DMA((6,))],
        compiler_params=PARAMS,
        name="begin",
    )(normed, gate_held, incoming, weight_out, second_send)


def transposed(gate_held, out_held):
    return pl.pallas_call(
        transpose_kernel,
        in_specs=[WHOLE] * 2,
        out_specs=[WHOLE] * 2,
        out_shape=[
            pltpu.VMEM(gate_held.shape[::-1], jnp.bfloat16),
            pltpu.VMEM(out_held.shape[::-1], jnp.bfloat16),
        ],
        compiler_params=PARAMS,
        name="transposed",
    )(gate_held, out_held)


def diagonal_blocks(matrix, count):
    rows, columns = matrix.shape[0] // count, matrix.shape[1] // count
    return jnp.stack(
        [
            matrix[k * rows : (k + 1) * rows, k * columns : (k + 1) * columns]
            for k in range(count)
        ]
    )


def per_device(section_inputs, cotangent, gain, w_gate, w_out, mix_first, mix_second):
    inputs = section_inputs[0]
    gain_row = gain[0]
    row_count, _ = inputs.shape
    local_blocks, block_rows = mix_first.shape[1:3]
    seq_count = lax.axis_size("seq")
    section_count = lax.axis_size("pipe")
    section_index = lax.axis_index("pipe")
    me = lax.axis_index("seq")
    order = Order(row_count, local_blocks, block_rows, seq_count)

    normed, inv_rms, kept, give, first_recv, second_send, second_recv, gate_held = prepare(
        order, me[None], inputs, gain, mix_first[0], mix_second[0], w_gate[0]
    )
    got_moved = swap(give, 1)
    mix_factor, slope, delta_hidden, delta_mix, kept_mix, give_mix, out_held = begin(
        normed, gate_held, cotangent, w_out[0], second_send
    )
    got_mid = swap(give_mix, 1)
    kept, got_moved, kept_mix = lax.optimization_barrier((kept, got_moved, kept_mix))
    moved = chip_exchange(kept, got_moved, seq_count)
    delta_mid = chip_exchange(kept_mix, got_mid, seq_count)
    gate_factor = dot(second_recv, moved) * slope

    unit_rows = inputs.astype(jnp.float32) * inv_rms
    incoming = cotangent
    gate_turned = None
    out_turned = None
    outgoing_kept = jnp.zeros_like(cotangent)
    first_kept = jnp.zeros((row_count, row_count), jnp.float32)
    second_kept = jnp.zeros((row_count, row_count), jnp.float32)
    for tick_index in range(section_count):
        sender = section_count - 1 - tick_index
        active = section_index == sender
        if tick_index > 0:
            delta_hidden = dot(incoming, out_turned)
            delta_mix = (delta_hidden * mix_factor).astype(jnp.bfloat16)
            send = dot(second_send, delta_mix).astype(jnp.bfloat16)
            kept_mix = send[: row_count // 2]
            delta_mid = chip_exchange(kept_mix, swap(send[row_count // 2 :], 1), seq_count)
        delta_gate = (delta_hidden * gate_factor).astype(jnp.bfloat16)
        gate_back = dot(delta_gate, gate_turned) if tick_index else dot_rows(delta_gate, gate_held)
        first_back = dot(first_recv, delta_mid)
        delta_norm = (first_back + gate_back) * gain_row
        centred = delta_norm - unit_rows * jnp.mean(delta_norm * unit_rows, axis=-1, keepdims=True)
        outgoing = (incoming.astype(jnp.float32) + inv_rms * centred).astype(jnp.bfloat16)
        if tick_index == 0:
            outgoing, gate_held, out_held = lax.optimization_barrier(
                (outgoing, gate_held, out_held)
            )
            gate_turned, out_turned = transposed(gate_held, out_held)
        if sender > 0:
            incoming = lax.ppermute(outgoing, "pipe", [(sender, sender - 1)])
        outgoing_kept = jnp.where(active, outgoing, outgoing_kept)
        first_kept = jnp.where(active, dot_rows(delta_mid, normed), first_kept)
        second_kept = jnp.where(active, dot_rows(delta_mix, moved), second_kept)

    position = jnp.arange(row_count)
    partner = order.recv_partner(position)

    def unpermuted(rows, matrix):
        return jnp.dot(
            (rows[:, None] == position[None, :]).astype(jnp.float32).T,
            matrix,
            precision=lax.Precision.HIGHEST,
            preferred_element_type=jnp.float32,
        )

    grad_first = diagonal_blocks(
        unpermuted(order.first_rows(me, partner, position), first_kept), local_blocks
    )
    grad_second = diagonal_blocks(
        unpermuted(order.second_rows(me, partner, position), second_kept.T).T, local_blocks
    )
    return (outgoing_kept[None], grad_first[None], grad_second[None])


def solution(mesh):
    placed = (
        P("pipe", "seq", None),
        P("seq", None),
        P("pipe", None),
        P("pipe", None, None),
        P("pipe", None, None),
        P("pipe", "seq", None, None),
        P("pipe", "seq", None, None),
    )
    return jax.shard_map(
        per_device,
        mesh=mesh,
        in_specs=placed,
        out_specs=(
            P("pipe", "seq", None),
            P("pipe", "seq", None, None),
            P("pipe", "seq", None, None),
        ),
        check_vma=False,
    )
```

```python
import functools

import jax
import jax.numpy as jnp
from jax import lax
from jax.experimental import pallas as pl
from jax.experimental.pallas import tpu as pltpu
from jax.sharding import PartitionSpec as P

ROWS_BY_ROWS = (((1,), (1,)), ((), ()))
WHOLE = pl.BlockSpec(memory_space=pltpu.VMEM)
ANYWHERE = pl.BlockSpec(memory_space=pl.ANY)
SCALAR = pl.BlockSpec(memory_space=pltpu.SMEM)
PARAMS = pltpu.CompilerParams(vmem_limit_bytes=12 << 20)


def in_hbm(array):
    return pltpu.with_memory_space_constraint(array, pltpu.HBM)


def dot(left, right):
    return jnp.dot(left, right, preferred_element_type=jnp.float32)


def dot_rows(left, right):
    return lax.dot_general(left, right, ROWS_BY_ROWS, preferred_element_type=jnp.float32)


def swap(block, offset):
    count = lax.axis_size("seq")
    return lax.ppermute(block, "seq", [(i, i ^ offset) for i in range(count)])


def chip_exchange(messages):
    return jnp.concatenate([messages[0]] + [swap(m, 2 * i) for i, m in enumerate(messages) if i])


def messages_of(kept, got, count):
    piece = kept.shape[0] // count
    parts = [slice(chip * piece, (chip + 1) * piece) for chip in range(count)]
    return [jnp.concatenate([kept[rows], got[rows]]) for rows in parts]


def chunks(size, count):
    return [slice(i * size // count, (i + 1) * size // count) for i in range(count)]


def block_diagonal(blocks):
    zero = jnp.zeros(blocks[0].shape, blocks[0].dtype)
    return jnp.concatenate(
        [
            jnp.concatenate([b if k == j else zero for j in range(len(blocks))], axis=1)
            for k, b in enumerate(blocks)
        ],
        axis=0,
    )


def log2(size):
    assert size & (size - 1) == 0
    return size.bit_length() - 1


class Order:
    def __init__(self, row_count, local_blocks, block_rows, seq_count):
        self.row_count = row_count
        self.local_blocks = local_blocks
        self.block_rows = block_rows
        self.seq_count = seq_count
        self.steps = block_rows // seq_count
        self.group = local_blocks * self.steps

    def recv_partner(self, position):
        return position >> log2(self.group)

    def send_partner(self, position):
        chip = (position >> log2(self.group)) & (self.seq_count // 2 - 1)
        return (position >> log2(self.row_count // 2)) + 2 * chip

    def block(self, position):
        return (position >> log2(self.steps)) & (self.local_blocks - 1)

    def first_rows(self, me, partner, position):
        step = position & (self.steps - 1)
        return self.block(position) * self.block_rows + (me ^ partner) * self.steps + step

    def second_rows(self, me, partner, position):
        step = position & (self.steps - 1)
        device = me ^ partner
        return (step * self.seq_count + device) * self.local_blocks + self.block(position)


def begin_kernel(
    order, x_hbm, gain_hbm, first_hbm, second_hbm, gate_hbm, incoming_hbm, out_hbm,
    normed_ref, inv_ref, first_recv_ref, second_send_ref, second_recv_ref,
    mix_factor_ref, slope_ref, hidden_ref, mix_ref, keep_ref, give_ref,
    x_ref, gain_ref, first_ref, second_ref, gate_ref, incoming_ref, out_ref, sems,
):
    parts = chunks(out_hbm.shape[0], sems.shape[0] - 6)
    pairs = [(x_hbm, x_ref), (first_hbm, first_ref), (second_hbm, second_ref), (gain_hbm, gain_ref)]
    pairs += [(gate_hbm, gate_ref), (incoming_hbm, incoming_ref)]
    pairs += [(out_hbm.at[rows], out_ref.at[rows]) for rows in parts]
    copies = [pltpu.make_async_copy(*pair, sems.at[i]) for i, pair in enumerate(pairs)]
    for copy in copies:
        copy.start()
    me = lax.axis_index("seq")
    square = (order.row_count, order.row_count)
    down = lax.broadcasted_iota(jnp.int32, square, 0)
    across = lax.broadcasted_iota(jnp.int32, square, 1)

    def one_hot(matches):
        return jnp.where(matches, 1.0, 0.0).astype(jnp.bfloat16)

    def rounded(left, right):
        return dot(left, right).astype(jnp.bfloat16)

    for copy in copies[:4]:
        copy.wait()
    first = block_diagonal([first_ref[k].astype(jnp.float32) for k in range(order.local_blocks)])
    second = block_diagonal([second_ref[k].astype(jnp.float32) for k in range(order.local_blocks)])
    sent, received = order.send_partner(down), order.recv_partner(across)
    first_send = rounded(
        one_hot(order.first_rows(me, sent, down) == across), first.astype(jnp.bfloat16)
    )
    second_send_ref[...] = rounded(
        one_hot(order.second_rows(me, sent, down) == across), second.T.astype(jnp.bfloat16)
    )
    first_recv_ref[...] = rounded(
        first.T.astype(jnp.bfloat16), one_hot(order.first_rows(me, received, across) == down)
    )
    second_recv_ref[...] = rounded(
        second.astype(jnp.bfloat16), one_hot(order.second_rows(me, received, across) == down)
    )
    features = x_ref[...].astype(jnp.float32)
    inv_rms = lax.rsqrt(jnp.mean(features * features, axis=-1, keepdims=True) + 1e-06)
    inv_ref[...] = inv_rms
    normed = (features * inv_rms * gain_ref[...]).astype(jnp.bfloat16)
    normed_ref[...] = normed

    def place(send, stream, columns):
        half = order.row_count // 2
        piece = half // (order.seq_count // 2)
        for row in range(0, half, piece):
            rows = slice(2 * row + stream * piece, 2 * row + (stream + 1) * piece)
            keep_ref[rows, columns] = send[row : row + piece]
            give_ref[rows, columns] = send[half + row : half + row + piece]

    place(rounded(first_send, normed), 0, slice(None))
    copies[4].wait()
    gate_pre = dot(normed, gate_ref[...])
    sigma = jax.nn.sigmoid(gate_pre)
    mix_factor_ref[...] = gate_pre * sigma
    slope_ref[...] = sigma * (1.0 + gate_pre * (1.0 - sigma))
    copies[5].wait()
    for columns, copy in zip(parts, copies[6:]):
        copy.wait()
        hidden = dot_rows(incoming_ref[...], out_ref[columns])
        hidden_ref[:, columns] = hidden
        mix = (hidden * mix_factor_ref[:, columns]).astype(jnp.bfloat16)
        mix_ref[:, columns] = mix
        place(rounded(second_send_ref[...], mix), 1, columns)


def pack_kernel(count, *refs):
    kept_ref, got_ref, outs = refs[0], refs[1], refs[-count:]
    piece = kept_ref.shape[0] // count
    for chip, out_ref in enumerate(outs):
        rows = slice(chip * piece, (chip + 1) * piece)
        out_ref[:piece] = kept_ref[rows]
        out_ref[piece:] = got_ref[rows]


def packed(kept, got, count):
    piece = jax.ShapeDtypeStruct((2 * kept.shape[0] // count, kept.shape[1]), kept.dtype)
    return pl.pallas_call(
        functools.partial(pack_kernel, count),
        in_specs=[WHOLE] * 2,
        out_specs=[WHOLE] * count,
        out_shape=[piece] * count,
        compiler_params=PARAMS,
        name="packed",
    )(kept, got)


def finish_kernel(
    count, *refs,
):
    messages, refs = refs[:count], refs[count:]
    (
        second_recv_ref, first_recv_ref, slope_ref, hidden_ref, gate_ref, gain_ref,
        x_ref, inv_ref, incoming_ref, moved_ref, mid_ref, gate_factor_ref, outgoing_ref,
    ) = refs
    piece = messages[0].shape[0] // 4
    for chip, message in enumerate(messages):
        for core in range(2):
            rows = slice((2 * chip + core) * piece, (2 * chip + core + 1) * piece)
            moved_ref[rows] = message[2 * core * piece : (2 * core + 1) * piece]
            mid_ref[rows] = message[(2 * core + 1) * piece : (2 * core + 2) * piece]
    gate_factor = dot(second_recv_ref[...], moved_ref[...]) * slope_ref[...]
    gate_factor_ref[...] = gate_factor
    delta_gate = (hidden_ref[...] * gate_factor).astype(jnp.bfloat16)
    gate_back = dot(delta_gate, gate_ref[...])
    first_back = dot(first_recv_ref[...], mid_ref[...])
    outgoing_ref[...] = outgoing_of(
        gate_back, first_back, gain_ref[...], x_ref[...], inv_ref[...], incoming_ref[...]
    )


def outgoing_of(gate_back, first_back, gain, inputs, inv_rms, incoming):
    delta_norm = (first_back + gate_back) * gain
    unit_rows = inputs.astype(jnp.float32) * inv_rms
    centred = delta_norm - unit_rows * jnp.mean(delta_norm * unit_rows, axis=-1, keepdims=True)
    return (incoming.astype(jnp.float32) + inv_rms * centred).astype(jnp.bfloat16)


def finish(messages, *operands):
    row_count, width = operands[-1].shape
    return pl.pallas_call(
        functools.partial(finish_kernel, len(messages)),
        in_specs=[WHOLE] * (len(messages) + len(operands)),
        out_specs=[WHOLE] * 4,
        out_shape=[
            jax.ShapeDtypeStruct((row_count, width), jnp.bfloat16),
            jax.ShapeDtypeStruct((row_count, width), jnp.bfloat16),
            jax.ShapeDtypeStruct((row_count, width), jnp.float32),
            jax.ShapeDtypeStruct((row_count, width), jnp.bfloat16),
        ],
        compiler_params=PARAMS,
        name="finish",
    )(*messages, *operands)


def transpose_kernel(weight_hbm, after_ref, turned_ref, held, sems):
    parts = chunks(held.shape[0], sems.shape[0])
    copies = [
        pltpu.make_async_copy(weight_hbm.at[rows], held.at[rows], sems.at[i])
        for i, rows in enumerate(parts)
    ]
    for copy in copies:
        copy.start()
    for rows, copy in zip(parts, copies):
        copy.wait()
        turned_ref[:, rows] = held[rows].T


def begin(order, *operands):
    row_count, width = operands[0].shape
    square = jax.ShapeDtypeStruct((row_count, row_count), jnp.bfloat16)
    short = jax.ShapeDtypeStruct((row_count, width), jnp.bfloat16)
    full = jax.ShapeDtypeStruct((row_count, width), jnp.float32)
    column = jax.ShapeDtypeStruct((row_count, 1), jnp.float32)
    return pl.pallas_call(
        functools.partial(begin_kernel, order),
        in_specs=[ANYWHERE] * len(operands),
        out_specs=[WHOLE] * 11,
        out_shape=[short, column, square, square, square, full, full, full, short, short, short],
        scratch_shapes=[pltpu.VMEM(o.shape, o.dtype) for o in operands]
        + [pltpu.SemaphoreType.DMA((9,))],
        compiler_params=pltpu.CompilerParams(vmem_limit_bytes=20 << 20),
        name="begin",
    )(*[in_hbm(o) for o in operands])


def transposed(weight, after):
    return pl.pallas_call(
        transpose_kernel,
        in_specs=[ANYWHERE, ANYWHERE],
        out_specs=WHOLE,
        out_shape=pltpu.VMEM(weight.shape[::-1], jnp.bfloat16),
        scratch_shapes=[pltpu.VMEM(weight.shape, weight.dtype), pltpu.SemaphoreType.DMA((6,))],
        compiler_params=PARAMS,
        name="transposed",
    )(in_hbm(weight), after)


def diagonal_blocks(matrix, count):
    rows, columns = matrix.shape[0] // count, matrix.shape[1] // count
    return jnp.stack(
        [
            matrix[k * rows : (k + 1) * rows, k * columns : (k + 1) * columns]
            for k in range(count)
        ]
    )


def per_device(section_inputs, cotangent, gain, w_gate, w_out, mix_first, mix_second):
    inputs = section_inputs[0]
    gain_row = gain[0]
    row_count, _ = inputs.shape
    local_blocks, block_rows = mix_first.shape[1:3]
    seq_count = lax.axis_size("seq")
    section_count = lax.axis_size("pipe")
    section_index = lax.axis_index("pipe")
    me = lax.axis_index("seq")
    order = Order(row_count, local_blocks, block_rows, seq_count)

    (
        normed, inv_rms, first_recv, second_send, second_recv,
        mix_factor, slope, delta_hidden, delta_mix, kept, give,
    ) = begin(
        order, inputs, gain, mix_first[0], mix_second[0], w_gate[0], cotangent, w_out[0]
    )
    messages = packed(kept, swap(give, 1), seq_count // 2)
    gate_turned = transposed(w_gate[0], messages[-1])
    messages = [messages[0]] + [swap(m, 2 * i) for i, m in enumerate(messages) if i]
    moved, delta_mid, gate_factor, outgoing = finish(
        messages, second_recv, first_recv, slope, delta_hidden, gate_turned, gain,
        inputs, inv_rms, cotangent,
    )
    out_turned = transposed(w_out[0], outgoing)

    outgoing_kept = outgoing
    first_kept = dot_rows(delta_mid, normed)
    second_kept = dot_rows(delta_mix, moved)
    for sender in reversed(range(section_count - 1)):
        active = section_index == sender
        incoming = lax.ppermute(outgoing, "pipe", [(sender + 1, sender)])
        delta_hidden = dot(incoming, out_turned)
        delta_mix = (delta_hidden * mix_factor).astype(jnp.bfloat16)
        send = dot(second_send, delta_mix).astype(jnp.bfloat16)
        kept_mix = send[: row_count // 2]
        got_mix = swap(send[row_count // 2 :], 1)
        delta_mid = chip_exchange(messages_of(kept_mix, got_mix, seq_count // 2))
        delta_gate = (delta_hidden * gate_factor).astype(jnp.bfloat16)
        gate_back = dot(delta_gate, gate_turned)
        first_back = dot(first_recv, delta_mid)
        outgoing = outgoing_of(gate_back, first_back, gain_row, inputs, inv_rms, incoming)
        outgoing_kept = jnp.where(active, outgoing, outgoing_kept)
        first_kept = jnp.where(active, dot_rows(delta_mid, normed), first_kept)
        second_kept = jnp.where(active, dot_rows(delta_mix, moved), second_kept)

    position = jnp.arange(row_count)
    partner = order.recv_partner(position)

    def unpermuted(rows, matrix):
        return jnp.dot(
            (rows[:, None] == position[None, :]).astype(jnp.float32).T,
            matrix,
            precision=lax.Precision.HIGHEST,
            preferred_element_type=jnp.float32,
        )

    grad_first = diagonal_blocks(
        unpermuted(order.first_rows(me, partner, position), first_kept), local_blocks
    )
    grad_second = diagonal_blocks(
        unpermuted(order.second_rows(me, partner, position), second_kept.T).T, local_blocks
    )
    return (outgoing_kept[None], grad_first[None], grad_second[None])


def solution(mesh):
    placed = (
        P("pipe", "seq", None),
        P("seq", None),
        P("pipe", None),
        P("pipe", None, None),
        P("pipe", None, None),
        P("pipe", "seq", None, None),
        P("pipe", "seq", None, None),
    )
    return jax.shard_map(
        per_device,
        mesh=mesh,
        in_specs=placed,
        out_specs=(
            P("pipe", "seq", None),
            P("pipe", "seq", None, None),
            P("pipe", "seq", None, None),
        ),
        check_vma=False,
    )
```

```python
import functools

import jax
import jax.numpy as jnp
from jax import lax
from jax.experimental import pallas as pl
from jax.experimental.pallas import tpu as pltpu
from jax.sharding import PartitionSpec as P

ROWS_BY_ROWS = (((1,), (1,)), ((), ()))
WHOLE = pl.BlockSpec(memory_space=pltpu.VMEM)
ANYWHERE = pl.BlockSpec(memory_space=pl.ANY)


def granted(mebibytes):
    return pltpu.CompilerParams(vmem_limit_bytes=mebibytes << 20)


def in_hbm(array):
    return pltpu.with_memory_space_constraint(array, pltpu.HBM)


def array_of(shape, dtype):
    return jax.ShapeDtypeStruct(shape, dtype)


def dot(left, right):
    return jnp.dot(left, right, preferred_element_type=jnp.float32)


def dot_rows(left, right):
    return lax.dot_general(left, right, ROWS_BY_ROWS, preferred_element_type=jnp.float32)


def swap(block, offset):
    count = lax.axis_size("seq")
    return lax.ppermute(block, "seq", [(i, i ^ offset) for i in range(count)])


def chunks(size, count):
    return [slice(i * size // count, (i + 1) * size // count) for i in range(count)]


def log2(size):
    assert size & (size - 1) == 0
    return size.bit_length() - 1


class Order:
    def __init__(self, row_count, local_blocks, block_rows, seq_count):
        self.row_count = row_count
        self.local_blocks = local_blocks
        self.block_rows = block_rows
        self.seq_count = seq_count
        self.chips = seq_count // 2
        self.steps = block_rows // seq_count
        self.piece = local_blocks * self.steps

    def rows(self, group, count=1):
        return slice(group * self.piece, (group + count) * self.piece)

    def sent(self, position):
        group = position >> log2(self.piece)
        return (group >> log2(self.chips)) + 2 * (group & (self.chips - 1))

    def received(self, position):
        return position >> log2(self.piece)

    def first_rows(self, me, partner, position):
        block = (position >> log2(self.steps)) & (self.local_blocks - 1)
        step = position & (self.steps - 1)
        return block * self.block_rows + (me ^ partner) * self.steps + step

    def second_rows(self, me, partner, position):
        block = (position >> log2(self.steps)) & (self.local_blocks - 1)
        step = position & (self.steps - 1)
        return (step * self.seq_count + (me ^ partner)) * self.local_blocks + block

    def exchange(self, kept, give, streams=1):
        got = swap(give, 1)
        arrived = []
        for chip in range(self.chips):
            rows = self.rows(chip * streams, streams)
            message = jnp.concatenate([kept[rows], got[rows]])
            arrived.append(swap(message, 2 * chip) if chip else message)
        return arrived


def block_diagonal(blocks):
    zero = jnp.zeros(blocks[0].shape, blocks[0].dtype)
    return jnp.concatenate(
        [
            jnp.concatenate([b if k == j else zero for j in range(len(blocks))], axis=1)
            for k, b in enumerate(blocks)
        ],
        axis=0,
    )


def positions(order):
    square = (order.row_count, order.row_count)
    return lax.broadcasted_iota(jnp.int32, square, 0), lax.broadcasted_iota(jnp.int32, square, 1)


def one_hot(matches, dtype=jnp.bfloat16):
    return jnp.where(matches, 1.0, 0.0).astype(dtype)


def rounded(left, right):
    return dot(left, right).astype(jnp.bfloat16)


def begin_kernel(
    order, x_hbm, gain_hbm, first_hbm, second_hbm, gate_hbm, incoming_hbm, out_hbm,
    normed_ref, inv_ref, first_recv_ref, second_send_ref, second_recv_ref,
    mix_factor_ref, slope_ref, hidden_ref, keep_ref, give_ref,
    x_ref, gain_ref, first_ref, second_ref, gate_ref, incoming_ref, out_ref, sems,
):
    parts = chunks(out_hbm.shape[0], sems.shape[0] - 6)
    pairs = [(x_hbm, x_ref), (first_hbm, first_ref), (second_hbm, second_ref), (gain_hbm, gain_ref)]
    pairs += [(gate_hbm, gate_ref), (incoming_hbm, incoming_ref)]
    pairs += [(out_hbm.at[rows], out_ref.at[rows]) for rows in parts]
    copies = [pltpu.make_async_copy(*pair, sems.at[i]) for i, pair in enumerate(pairs)]
    for copy in copies[:5]:
        copy.start()
    active = lax.axis_index("pipe") == lax.axis_size("pipe") - 1

    @pl.when(active)
    def _():
        for copy in copies[5:]:
            copy.start()

    me = lax.axis_index("seq")
    down, across = positions(order)
    for copy in copies[:4]:
        copy.wait()
    first = block_diagonal([first_ref[k].astype(jnp.float32) for k in range(order.local_blocks)])
    second = block_diagonal([second_ref[k].astype(jnp.float32) for k in range(order.local_blocks)])
    sent, received = order.sent(down), order.received(across)
    first_send = rounded(
        one_hot(order.first_rows(me, sent, down) == across), first.astype(jnp.bfloat16)
    )
    second_send_ref[...] = rounded(
        one_hot(order.second_rows(me, sent, down) == across), second.T.astype(jnp.bfloat16)
    )
    first_recv_ref[...] = rounded(
        first.T.astype(jnp.bfloat16), one_hot(order.first_rows(me, received, across) == down)
    )
    second_recv_ref[...] = rounded(
        second.astype(jnp.bfloat16), one_hot(order.second_rows(me, received, across) == down)
    )
    features = x_ref[...].astype(jnp.float32)
    inv_rms = lax.rsqrt(jnp.mean(features * features, axis=-1, keepdims=True) + 1e-06)
    inv_ref[...] = inv_rms
    normed = (features * inv_rms * gain_ref[...]).astype(jnp.bfloat16)
    normed_ref[...] = normed

    def place(send, stream, columns):
        for core, target in enumerate((keep_ref, give_ref)):
            for chip in range(order.chips):
                rows = order.rows(2 * chip + stream)
                target[rows, columns] = send[order.rows(core * order.chips + chip)]

    place(rounded(first_send, normed), 0, slice(None))
    copies[4].wait()
    gate_pre = dot(normed, gate_ref[...])
    sigma = jax.nn.sigmoid(gate_pre)
    mix_factor_ref[...] = gate_pre * sigma
    slope_ref[...] = sigma * (1.0 + gate_pre * (1.0 - sigma))

    @pl.when(active)
    def _():
        copies[5].wait()
        for columns, copy in zip(parts, copies[6:]):
            copy.wait()
            hidden = dot_rows(incoming_ref[...], out_ref[columns])
            hidden_ref[:, columns] = hidden
            mix = (hidden * mix_factor_ref[:, columns]).astype(jnp.bfloat16)
            place(rounded(second_send_ref[...], mix), 1, columns)

    @pl.when(jnp.logical_not(active))
    def _():
        hidden_ref[...] = jnp.zeros(hidden_ref.shape, hidden_ref.dtype)
        place(jnp.zeros(normed_ref.shape, normed_ref.dtype), 1, slice(None))


def begin(order, *operands):
    row_count, width = operands[0].shape
    square = array_of((row_count, row_count), jnp.bfloat16)
    short = array_of((row_count, width), jnp.bfloat16)
    full = array_of((row_count, width), jnp.float32)
    column = array_of((row_count, 1), jnp.float32)
    outs = [short, column, square, square, square, full, full, full, short, short]
    return pl.pallas_call(
        functools.partial(begin_kernel, order),
        in_specs=[ANYWHERE] * len(operands),
        out_specs=[WHOLE] * len(outs),
        out_shape=outs,
        scratch_shapes=[pltpu.VMEM(o.shape, o.dtype) for o in operands]
        + [pltpu.SemaphoreType.DMA((9,))],
        compiler_params=granted(13),
        name="begin",
    )(*[in_hbm(o) for o in operands])


def transpose_kernel(weight_hbm, after_ref, turned_ref, held, sems):
    parts = chunks(held.shape[0], sems.shape[0])
    copies = [
        pltpu.make_async_copy(weight_hbm.at[rows], held.at[rows], sems.at[i])
        for i, rows in enumerate(parts)
    ]
    for copy in copies:
        copy.start()
    for rows, copy in zip(parts, copies):
        copy.wait()
        turned_ref[:, rows] = held[rows].T


def transposed(weight, after):
    return pl.pallas_call(
        transpose_kernel,
        in_specs=[ANYWHERE, ANYWHERE],
        out_specs=WHOLE,
        out_shape=pltpu.VMEM(weight.shape[::-1], jnp.bfloat16),
        scratch_shapes=[pltpu.VMEM(weight.shape, weight.dtype), pltpu.SemaphoreType.DMA((6,))],
        compiler_params=granted(6),
        name="transposed",
    )(in_hbm(weight), after)


def outgoing_of(gate_back, first_back, gain, inputs, inv_rms, incoming):
    delta_norm = (first_back + gate_back) * gain
    unit_rows = inputs.astype(jnp.float32) * inv_rms
    centred = delta_norm - unit_rows * jnp.mean(delta_norm * unit_rows, axis=-1, keepdims=True)
    return (incoming.astype(jnp.float32) + inv_rms * centred).astype(jnp.bfloat16)


def finish_kernel(order, *refs):
    arrived, refs = refs[: order.chips], refs[order.chips :]
    (
        second_recv_ref, first_recv_ref, slope_ref, hidden_ref, gate_ref, gain_ref, x_ref, inv_ref,
        incoming_ref, moved_ref, mid_ref, gate_factor_ref, outgoing_ref,
    ) = refs
    for chip, message in enumerate(arrived):
        for core in range(2):
            for stream, target in enumerate((moved_ref, mid_ref)):
                target[order.rows(2 * chip + core)] = message[order.rows(2 * core + stream)]
    gate_factor = dot(second_recv_ref[...], moved_ref[...]) * slope_ref[...]
    gate_factor_ref[...] = gate_factor
    delta_gate = (hidden_ref[...] * gate_factor).astype(jnp.bfloat16)
    gate_back = dot(delta_gate, gate_ref[...])
    first_back = dot(first_recv_ref[...], mid_ref[...])
    outgoing_ref[...] = outgoing_of(
        gate_back, first_back, gain_ref[...], x_ref[...], inv_ref[...], incoming_ref[...]
    )


def finish(order, *operands):
    row_count, width = operands[-1].shape
    short = array_of((row_count, width), jnp.bfloat16)
    full = array_of((row_count, width), jnp.float32)
    return pl.pallas_call(
        functools.partial(finish_kernel, order),
        in_specs=[WHOLE] * len(operands),
        out_specs=[WHOLE] * 4,
        out_shape=[short, short, full, short],
        compiler_params=granted(4),
        name="finish",
    )(*operands)


def advance_kernel(
    mid_ref, first_recv_ref, gate_back_ref, gain_ref, x_ref, inv_ref, incoming_ref, outgoing_ref
):
    first_back = dot(first_recv_ref[...], mid_ref[...])
    outgoing_ref[...] = outgoing_of(
        gate_back_ref[...], first_back, gain_ref[...], x_ref[...], inv_ref[...], incoming_ref[...]
    )


def advance(*operands):
    return pl.pallas_call(
        advance_kernel,
        in_specs=[WHOLE] * len(operands),
        out_specs=WHOLE,
        out_shape=array_of(operands[0].shape, jnp.bfloat16),
        compiler_params=granted(4),
        name="advance",
    )(*operands)


def keep_kernel(
    section, outgoing_ref, mid_ref, mix_ref, normed_ref, moved_ref, *refs
):
    kept, new = refs[:3], refs[3:]
    active = lax.axis_index("pipe") == section

    @pl.when(active)
    def _():
        new[0][...] = outgoing_ref[...]
        new[1][...] = dot_rows(mid_ref[...], normed_ref[...])
        new[2][...] = dot_rows(mix_ref[...], moved_ref[...])

    @pl.when(jnp.logical_not(active))
    def _():
        for old_ref, new_ref in zip(kept, new):
            new_ref[...] = old_ref[...]


def keep(section, kept, *operands):
    count = len(operands)
    return pl.pallas_call(
        functools.partial(keep_kernel, section),
        in_specs=[WHOLE] * (count + 3),
        out_specs=[WHOLE] * 3,
        out_shape=[array_of(k.shape, k.dtype) for k in kept],
        input_output_aliases={count + i: i for i in range(3)},
        compiler_params=granted(2),
        name="keep",
    )(*operands, *kept)


def close_kernel(
    order, mid_ref, mix_ref, moved_ref, first_recv_ref, gate_back_ref, gain_ref, x_ref, inv_ref, incoming_ref, normed_ref,
    outgoing_kept_ref, first_kept_ref, second_kept_ref, outgoing_ref, first_ref, second_ref,
):
    active = lax.axis_index("pipe") == 0
    first_back = dot(first_recv_ref[...], mid_ref[...])
    outgoing = outgoing_of(
        gate_back_ref[...], first_back, gain_ref[...], x_ref[...], inv_ref[...], incoming_ref[...]
    )
    outgoing_ref[...] = jnp.where(active, outgoing, outgoing_kept_ref[...])
    first = jnp.where(active, dot_rows(mid_ref[...], normed_ref[...]), first_kept_ref[...])
    second = jnp.where(active, dot_rows(mix_ref[...], moved_ref[...]), second_kept_ref[...])
    me = lax.axis_index("seq")
    down, across = positions(order)

    def exact(left, right):
        return jnp.dot(
            left, right, precision=lax.Precision.HIGHEST, preferred_element_type=jnp.float32
        )

    to_first = order.first_rows(me, order.received(across), across) == down
    to_second = order.second_rows(me, order.received(down), down) == across
    first = exact(one_hot(to_first, jnp.float32), first)
    second = exact(second, one_hot(to_second, jnp.float32))
    for k, rows in enumerate(chunks(order.row_count, order.local_blocks)):
        first_ref[k] = first[rows, rows]
        second_ref[k] = second[rows, rows]


def close(order, *operands):
    row_count, width = operands[0].shape
    blocks = array_of((order.local_blocks, order.block_rows, order.block_rows), jnp.float32)
    return pl.pallas_call(
        functools.partial(close_kernel, order),
        in_specs=[WHOLE] * len(operands),
        out_specs=[WHOLE] * 3,
        out_shape=[array_of((row_count, width), jnp.bfloat16), blocks, blocks],
        compiler_params=granted(4),
        name="close",
    )(*operands)


def per_device(section_inputs, cotangent, gain, w_gate, w_out, mix_first, mix_second):
    inputs = section_inputs[0]
    local_blocks, block_rows = mix_first.shape[1:3]
    section_count = lax.axis_size("pipe")
    order = Order(inputs.shape[0], local_blocks, block_rows, lax.axis_size("seq"))

    (
        normed, inv_rms, first_recv, second_send, second_recv,
        mix_factor, slope, delta_hidden, kept, give,
    ) = begin(
        order, inputs, gain, mix_first[0], mix_second[0], w_gate[0], cotangent, w_out[0]
    )
    arrived = order.exchange(kept, give, streams=2)
    gate_turned = transposed(w_gate[0], arrived[0])
    moved, delta_mid, gate_factor, outgoing = finish(
        order, *arrived, second_recv, first_recv, slope, delta_hidden, gate_turned, gain,
        inputs, inv_rms, cotangent,
    )
    out_turned = transposed(w_out[0], outgoing)

    delta_mix = (delta_hidden * mix_factor).astype(jnp.bfloat16)
    kept = (outgoing, dot_rows(delta_mid, normed), dot_rows(delta_mix, moved))
    for sender in reversed(range(section_count - 1)):
        incoming = lax.ppermute(outgoing, "pipe", [(sender + 1, sender)])
        delta_hidden = dot(incoming, out_turned)
        delta_mix = (delta_hidden * mix_factor).astype(jnp.bfloat16)
        send = rounded(second_send, delta_mix)
        delta_mid = jnp.concatenate(order.exchange(*jnp.split(send, 2)))
        delta_gate = (delta_hidden * gate_factor).astype(jnp.bfloat16)
        gate_back = dot(delta_gate, gate_turned)
        if sender > 0:
            outgoing = advance(delta_mid, first_recv, gate_back, gain, inputs, inv_rms, incoming)
            kept = keep(sender, kept, outgoing, delta_mid, delta_mix, normed, moved)
    grad_inputs, grad_first, grad_second = close(
        order, delta_mid, delta_mix, moved, first_recv, gate_back, gain, inputs, inv_rms, incoming,
        normed, *kept,
    )
    return (grad_inputs[None], grad_first[None], grad_second[None])


def solution(mesh):
    placed = (
        P("pipe", "seq", None),
        P("seq", None),
        P("pipe", None),
        P("pipe", None, None),
        P("pipe", None, None),
        P("pipe", "seq", None, None),
        P("pipe", "seq", None, None),
    )
    return jax.shard_map(
        per_device,
        mesh=mesh,
        in_specs=placed,
        out_specs=(
            P("pipe", "seq", None),
            P("pipe", "seq", None, None),
            P("pipe", "seq", None, None),
        ),
        check_vma=False,
    )
```

```python
import functools

import jax
import jax.numpy as jnp
from jax import lax
from jax.experimental import pallas as pl
from jax.experimental.pallas import tpu as pltpu
from jax.sharding import PartitionSpec as P

ROWS_BY_ROWS = (((1,), (1,)), ((), ()))
WHOLE = pl.BlockSpec(memory_space=pltpu.VMEM)
ANYWHERE = pl.BlockSpec(memory_space=pl.ANY)


def granted(mebibytes):
    return pltpu.CompilerParams(vmem_limit_bytes=mebibytes << 20)


def in_hbm(array):
    return pltpu.with_memory_space_constraint(array, pltpu.HBM)


def array_of(shape, dtype):
    return jax.ShapeDtypeStruct(shape, dtype)


def dot(left, right):
    return jnp.dot(left, right, preferred_element_type=jnp.float32)


def dot_rows(left, right):
    return lax.dot_general(left, right, ROWS_BY_ROWS, preferred_element_type=jnp.float32)


def swap(block, offset):
    count = lax.axis_size("seq")
    return lax.ppermute(block, "seq", [(i, i ^ offset) for i in range(count)])


def passed_down(block, sender):
    count = lax.axis_size("pipe")
    pairs = [(sender, sender - 1)]
    if count % 2 == 0 and sender % 2 == 1:
        pairs = [(i, i ^ 1) for i in range(count)]
    return lax.ppermute(block, "pipe", pairs)


def chunks(size, count):
    return [slice(i * size // count, (i + 1) * size // count) for i in range(count)]


def log2(size):
    assert size & (size - 1) == 0
    return size.bit_length() - 1


class Order:
    def __init__(self, row_count, local_blocks, block_rows, seq_count):
        self.row_count = row_count
        self.local_blocks = local_blocks
        self.block_rows = block_rows
        self.seq_count = seq_count
        self.chips = seq_count // 2
        self.steps = block_rows // seq_count
        self.piece = local_blocks * self.steps

    def rows(self, group, count=1):
        return slice(group * self.piece, (group + count) * self.piece)

    def sent(self, position):
        group = position >> log2(self.piece)
        return (group >> log2(self.chips)) + 2 * (group & (self.chips - 1))

    def received(self, position):
        return position >> log2(self.piece)

    def first_rows(self, me, partner, position):
        block = (position >> log2(self.steps)) & (self.local_blocks - 1)
        step = position & (self.steps - 1)
        return block * self.block_rows + (me ^ partner) * self.steps + step

    def second_rows(self, me, partner, position):
        block = (position >> log2(self.steps)) & (self.local_blocks - 1)
        step = position & (self.steps - 1)
        return (step * self.seq_count + (me ^ partner)) * self.local_blocks + block

    def exchange(self, kept, give, streams=1):
        got = swap(give, 1)
        arrived = []
        for chip in range(self.chips):
            rows = self.rows(chip * streams, streams)
            message = jnp.concatenate([kept[rows], got[rows]])
            arrived.append(swap(message, 2 * chip) if chip else message)
        return arrived


def block_diagonal(blocks):
    zero = jnp.zeros(blocks[0].shape, blocks[0].dtype)
    return jnp.concatenate(
        [
            jnp.concatenate([b if k == j else zero for j in range(len(blocks))], axis=1)
            for k, b in enumerate(blocks)
        ],
        axis=0,
    )


def positions(order):
    square = (order.row_count, order.row_count)
    return lax.broadcasted_iota(jnp.int32, square, 0), lax.broadcasted_iota(jnp.int32, square, 1)


def one_hot(matches, dtype=jnp.bfloat16):
    return jnp.where(matches, 1.0, 0.0).astype(dtype)


def rounded(left, right):
    return dot(left, right).astype(jnp.bfloat16)


def begin_kernel(
    order, x_hbm, gain_hbm, first_hbm, second_hbm, gate_hbm, incoming_hbm, out_hbm,
    normed_ref, inv_ref, first_recv_ref, second_send_ref, second_recv_ref,
    mix_factor_ref, slope_ref, hidden_ref, keep_ref, give_ref,
    x_ref, gain_ref, first_ref, second_ref, gate_ref, incoming_ref, out_ref, sems,
):
    parts = chunks(out_hbm.shape[0], sems.shape[0] - 6)
    pairs = [(x_hbm, x_ref), (first_hbm, first_ref), (second_hbm, second_ref), (gain_hbm, gain_ref)]
    pairs += [(gate_hbm, gate_ref), (incoming_hbm, incoming_ref)]
    pairs += [(out_hbm.at[rows], out_ref.at[rows]) for rows in parts]
    copies = [pltpu.make_async_copy(*pair, sems.at[i]) for i, pair in enumerate(pairs)]
    for copy in copies[:5]:
        copy.start()
    active = lax.axis_index("pipe") == lax.axis_size("pipe") - 1

    @pl.when(active)
    def _():
        for copy in copies[5:]:
            copy.start()

    me = lax.axis_index("seq")
    down, across = positions(order)
    for copy in copies[:4]:
        copy.wait()
    first = block_diagonal([first_ref[k].astype(jnp.float32) for k in range(order.local_blocks)])
    second = block_diagonal([second_ref[k].astype(jnp.float32) for k in range(order.local_blocks)])
    sent, received = order.sent(down), order.received(across)
    first_send = rounded(
        one_hot(order.first_rows(me, sent, down) == across), first.astype(jnp.bfloat16)
    )
    second_send_ref[...] = rounded(
        one_hot(order.second_rows(me, sent, down) == across), second.T.astype(jnp.bfloat16)
    )
    first_recv_ref[...] = rounded(
        first.T.astype(jnp.bfloat16), one_hot(order.first_rows(me, received, across) == down)
    )
    second_recv_ref[...] = rounded(
        second.astype(jnp.bfloat16), one_hot(order.second_rows(me, received, across) == down)
    )
    features = x_ref[...].astype(jnp.float32)
    inv_rms = lax.rsqrt(jnp.mean(features * features, axis=-1, keepdims=True) + 1e-06)
    inv_ref[...] = inv_rms
    normed = (features * inv_rms * gain_ref[...]).astype(jnp.bfloat16)
    normed_ref[...] = normed

    def place(send, stream, columns):
        for core, target in enumerate((keep_ref, give_ref)):
            for chip in range(order.chips):
                rows = order.rows(2 * chip + stream)
                target[rows, columns] = send[order.rows(core * order.chips + chip)]

    place(rounded(first_send, normed), 0, slice(None))
    copies[4].wait()
    gate_pre = dot(normed, gate_ref[...])
    sigma = jax.nn.sigmoid(gate_pre)
    mix_factor_ref[...] = gate_pre * sigma
    slope_ref[...] = sigma * (1.0 + gate_pre * (1.0 - sigma))

    @pl.when(active)
    def _():
        copies[5].wait()
        for columns, copy in zip(parts, copies[6:]):
            copy.wait()
            hidden = dot_rows(incoming_ref[...], out_ref[columns])
            hidden_ref[:, columns] = hidden
            mix = (hidden * mix_factor_ref[:, columns]).astype(jnp.bfloat16)
            place(rounded(second_send_ref[...], mix), 1, columns)

    @pl.when(jnp.logical_not(active))
    def _():
        hidden_ref[...] = jnp.zeros(hidden_ref.shape, hidden_ref.dtype)
        place(jnp.zeros(normed_ref.shape, normed_ref.dtype), 1, slice(None))


def begin(order, *operands):
    row_count, width = operands[0].shape
    square = array_of((row_count, row_count), jnp.bfloat16)
    short = array_of((row_count, width), jnp.bfloat16)
    full = array_of((row_count, width), jnp.float32)
    column = array_of((row_count, 1), jnp.float32)
    outs = [short, column, square, square, square, full, full, full, short, short]
    return pl.pallas_call(
        functools.partial(begin_kernel, order),
        in_specs=[ANYWHERE] * len(operands),
        out_specs=[WHOLE] * len(outs),
        out_shape=outs,
        scratch_shapes=[pltpu.VMEM(o.shape, o.dtype) for o in operands]
        + [pltpu.SemaphoreType.DMA((9,))],
        compiler_params=granted(13),
        name="begin",
    )(*[in_hbm(o) for o in operands])


def transpose_kernel(weight_hbm, after_ref, turned_ref, held, sems):
    parts = chunks(held.shape[0], sems.shape[0])
    copies = [
        pltpu.make_async_copy(weight_hbm.at[rows], held.at[rows], sems.at[i])
        for i, rows in enumerate(parts)
    ]
    for copy in copies:
        copy.start()
    for rows, copy in zip(parts, copies):
        copy.wait()
        turned_ref[:, rows] = held[rows].T


def transposed(weight, after):
    return pl.pallas_call(
        transpose_kernel,
        in_specs=[ANYWHERE, ANYWHERE],
        out_specs=WHOLE,
        out_shape=pltpu.VMEM(weight.shape[::-1], jnp.bfloat16),
        scratch_shapes=[pltpu.VMEM(weight.shape, weight.dtype), pltpu.SemaphoreType.DMA((6,))],
        compiler_params=granted(6),
        name="transposed",
    )(in_hbm(weight), after)


def outgoing_of(gate_back, first_back, gain, inputs, inv_rms, incoming):
    delta_norm = (first_back + gate_back) * gain
    unit_rows = inputs.astype(jnp.float32) * inv_rms
    centred = delta_norm - unit_rows * jnp.mean(delta_norm * unit_rows, axis=-1, keepdims=True)
    return (incoming.astype(jnp.float32) + inv_rms * centred).astype(jnp.bfloat16)


def finish_kernel(order, *refs):
    arrived, refs = refs[: order.chips], refs[order.chips :]
    (
        second_recv_ref, first_recv_ref, slope_ref, hidden_ref, gate_ref, gain_ref, x_ref, inv_ref,
        incoming_ref, moved_ref, mid_ref, gate_factor_ref, outgoing_ref,
    ) = refs
    for chip, message in enumerate(arrived):
        for core in range(2):
            for stream, target in enumerate((moved_ref, mid_ref)):
                target[order.rows(2 * chip + core)] = message[order.rows(2 * core + stream)]
    gate_factor = dot(second_recv_ref[...], moved_ref[...]) * slope_ref[...]
    gate_factor_ref[...] = gate_factor
    delta_gate = (hidden_ref[...] * gate_factor).astype(jnp.bfloat16)
    gate_back = dot(delta_gate, gate_ref[...])
    first_back = dot(first_recv_ref[...], mid_ref[...])
    outgoing_ref[...] = outgoing_of(
        gate_back, first_back, gain_ref[...], x_ref[...], inv_ref[...], incoming_ref[...]
    )


def finish(order, *operands):
    row_count, width = operands[-1].shape
    short = array_of((row_count, width), jnp.bfloat16)
    full = array_of((row_count, width), jnp.float32)
    return pl.pallas_call(
        functools.partial(finish_kernel, order),
        in_specs=[WHOLE] * len(operands),
        out_specs=[WHOLE] * 4,
        out_shape=[short, short, full, short],
        compiler_params=granted(4),
        name="finish",
    )(*operands)


def advance_kernel(
    mid_ref, first_recv_ref, gate_back_ref, gain_ref, x_ref, inv_ref, incoming_ref, outgoing_ref
):
    first_back = dot(first_recv_ref[...], mid_ref[...])
    outgoing_ref[...] = outgoing_of(
        gate_back_ref[...], first_back, gain_ref[...], x_ref[...], inv_ref[...], incoming_ref[...]
    )


def advance(*operands):
    return pl.pallas_call(
        advance_kernel,
        in_specs=[WHOLE] * len(operands),
        out_specs=WHOLE,
        out_shape=array_of(operands[0].shape, jnp.bfloat16),
        compiler_params=granted(4),
        name="advance",
    )(*operands)


def keep_kernel(
    section, outgoing_ref, mid_ref, mix_ref, normed_ref, moved_ref, *refs
):
    kept, new = refs[:3], refs[3:]
    active = lax.axis_index("pipe") == section

    @pl.when(active)
    def _():
        new[0][...] = outgoing_ref[...]
        new[1][...] = dot_rows(mid_ref[...], normed_ref[...])
        new[2][...] = dot_rows(mix_ref[...], moved_ref[...])

    @pl.when(jnp.logical_not(active))
    def _():
        for old_ref, new_ref in zip(kept, new):
            new_ref[...] = old_ref[...]


def keep(section, kept, *operands):
    count = len(operands)
    return pl.pallas_call(
        functools.partial(keep_kernel, section),
        in_specs=[WHOLE] * (count + 3),
        out_specs=[WHOLE] * 3,
        out_shape=[array_of(k.shape, k.dtype) for k in kept],
        input_output_aliases={count + i: i for i in range(3)},
        compiler_params=granted(2),
        name="keep",
    )(*operands, *kept)


def close_kernel(
    order, mid_ref, mix_ref, moved_ref, first_recv_ref, gate_back_ref, gain_ref, x_ref, inv_ref, incoming_ref, normed_ref,
    outgoing_kept_ref, first_kept_ref, second_kept_ref, outgoing_ref, first_ref, second_ref,
):
    active = lax.axis_index("pipe") == 0
    first_back = dot(first_recv_ref[...], mid_ref[...])
    outgoing = outgoing_of(
        gate_back_ref[...], first_back, gain_ref[...], x_ref[...], inv_ref[...], incoming_ref[...]
    )
    outgoing_ref[...] = jnp.where(active, outgoing, outgoing_kept_ref[...])
    first = jnp.where(active, dot_rows(mid_ref[...], normed_ref[...]), first_kept_ref[...])
    second = jnp.where(active, dot_rows(mix_ref[...], moved_ref[...]), second_kept_ref[...])
    me = lax.axis_index("seq")
    down, across = positions(order)

    def exact(left, right):
        return jnp.dot(
            left, right, precision=lax.Precision.HIGHEST, preferred_element_type=jnp.float32
        )

    to_first = order.first_rows(me, order.received(across), across) == down
    to_second = order.second_rows(me, order.received(down), down) == across
    first = exact(one_hot(to_first, jnp.float32), first)
    second = exact(second, one_hot(to_second, jnp.float32))
    for k, rows in enumerate(chunks(order.row_count, order.local_blocks)):
        first_ref[k] = first[rows, rows]
        second_ref[k] = second[rows, rows]


def close(order, *operands):
    row_count, width = operands[0].shape
    blocks = array_of((order.local_blocks, order.block_rows, order.block_rows), jnp.float32)
    return pl.pallas_call(
        functools.partial(close_kernel, order),
        in_specs=[WHOLE] * len(operands),
        out_specs=[WHOLE] * 3,
        out_shape=[array_of((row_count, width), jnp.bfloat16), blocks, blocks],
        compiler_params=granted(4),
        name="close",
    )(*operands)


def per_device(section_inputs, cotangent, gain, w_gate, w_out, mix_first, mix_second):
    inputs = section_inputs[0]
    local_blocks, block_rows = mix_first.shape[1:3]
    section_count = lax.axis_size("pipe")
    order = Order(inputs.shape[0], local_blocks, block_rows, lax.axis_size("seq"))

    (
        normed, inv_rms, first_recv, second_send, second_recv,
        mix_factor, slope, delta_hidden, kept, give,
    ) = begin(
        order, inputs, gain, mix_first[0], mix_second[0], w_gate[0], cotangent, w_out[0]
    )
    arrived = order.exchange(kept, give, streams=2)
    gate_turned = transposed(w_gate[0], arrived[0])
    moved, delta_mid, gate_factor, outgoing = finish(
        order, *arrived, second_recv, first_recv, slope, delta_hidden, gate_turned, gain,
        inputs, inv_rms, cotangent,
    )
    out_turned = transposed(w_out[0], outgoing)

    delta_mix = (delta_hidden * mix_factor).astype(jnp.bfloat16)
    kept = (outgoing, dot_rows(delta_mid, normed), dot_rows(delta_mix, moved))
    for sender in reversed(range(section_count - 1)):
        incoming = passed_down(outgoing, sender + 1)
        delta_hidden = dot(incoming, out_turned)
        delta_mix = (delta_hidden * mix_factor).astype(jnp.bfloat16)
        send = rounded(second_send, delta_mix)
        delta_mid = jnp.concatenate(order.exchange(*jnp.split(send, 2)))
        delta_gate = (delta_hidden * gate_factor).astype(jnp.bfloat16)
        gate_back = dot(delta_gate, gate_turned)
        if sender > 0:
            outgoing = advance(delta_mid, first_recv, gate_back, gain, inputs, inv_rms, incoming)
            kept = keep(sender, kept, outgoing, delta_mid, delta_mix, normed, moved)
    grad_inputs, grad_first, grad_second = close(
        order, delta_mid, delta_mix, moved, first_recv, gate_back, gain, inputs, inv_rms, incoming,
        normed, *kept,
    )
    return (grad_inputs[None], grad_first[None], grad_second[None])


def solution(mesh):
    placed = (
        P("pipe", "seq", None),
        P("seq", None),
        P("pipe", None),
        P("pipe", None, None),
        P("pipe", None, None),
        P("pipe", "seq", None, None),
        P("pipe", "seq", None, None),
    )
    return jax.shard_map(
        per_device,
        mesh=mesh,
        in_specs=placed,
        out_specs=(
            P("pipe", "seq", None),
            P("pipe", "seq", None, None),
            P("pipe", "seq", None, None),
        ),
        check_vma=False,
    )
```

```python
import functools

import jax
import jax.numpy as jnp
from jax import lax
from jax.experimental import pallas as pl
from jax.experimental.pallas import tpu as pltpu
from jax.sharding import PartitionSpec as P

ROWS_BY_ROWS = (((1,), (1,)), ((), ()))
WHOLE = pl.BlockSpec(memory_space=pltpu.VMEM)
ANYWHERE = pl.BlockSpec(memory_space=pl.ANY)
HALVES = 2


def granted(mebibytes):
    return pltpu.CompilerParams(vmem_limit_bytes=mebibytes << 20)


def in_hbm(array):
    return pltpu.with_memory_space_constraint(array, pltpu.HBM)


def array_of(shape, dtype):
    return jax.ShapeDtypeStruct(shape, dtype)


def dot(left, right):
    return jnp.dot(left, right, preferred_element_type=jnp.float32)


def dot_rows(left, right):
    return lax.dot_general(left, right, ROWS_BY_ROWS, preferred_element_type=jnp.float32)


def swap(block, offset):
    count = lax.axis_size("seq")
    return lax.ppermute(block, "seq", [(i, i ^ offset) for i in range(count)])


def passed_down(block, sender):
    count = lax.axis_size("pipe")
    pairs = [(sender, sender - 1)]
    if count % 2 == 0 and sender % 2 == 1:
        pairs = [(i, i ^ 1) for i in range(count)]
    return lax.ppermute(block, "pipe", pairs)


def chunks(size, count):
    return [slice(i * size // count, (i + 1) * size // count) for i in range(count)]


def log2(size):
    assert size & (size - 1) == 0
    return size.bit_length() - 1


class Order:
    def __init__(self, row_count, local_blocks, block_rows, seq_count):
        self.row_count = row_count
        self.local_blocks = local_blocks
        self.block_rows = block_rows
        self.seq_count = seq_count
        self.chips = seq_count // 2
        self.steps = block_rows // seq_count
        self.piece = local_blocks * self.steps

    def rows(self, group, count=1):
        return slice(group * self.piece, (group + count) * self.piece)

    def sent(self, position):
        group = position >> log2(self.piece)
        return (group >> log2(self.chips)) + 2 * (group & (self.chips - 1))

    def received(self, position):
        return position >> log2(self.piece)

    def first_rows(self, me, partner, position):
        block = (position >> log2(self.steps)) & (self.local_blocks - 1)
        step = position & (self.steps - 1)
        return block * self.block_rows + (me ^ partner) * self.steps + step

    def second_rows(self, me, partner, position):
        block = (position >> log2(self.steps)) & (self.local_blocks - 1)
        step = position & (self.steps - 1)
        return (step * self.seq_count + (me ^ partner)) * self.local_blocks + block

    def exchange(self, kept, give, streams=1):
        got = swap(give, 1)
        arrived = []
        for chip in range(self.chips):
            rows = self.rows(chip * streams, streams)
            message = jnp.concatenate([kept[rows], got[rows]])
            arrived.append(swap(message, 2 * chip) if chip else message)
        return arrived


def block_diagonal(blocks):
    zero = jnp.zeros(blocks[0].shape, blocks[0].dtype)
    return jnp.concatenate(
        [
            jnp.concatenate([b if k == j else zero for j in range(len(blocks))], axis=1)
            for k, b in enumerate(blocks)
        ],
        axis=0,
    )


def positions(order):
    square = (order.row_count, order.row_count)
    return lax.broadcasted_iota(jnp.int32, square, 0), lax.broadcasted_iota(jnp.int32, square, 1)


def one_hot(matches, dtype=jnp.bfloat16):
    return jnp.where(matches, 1.0, 0.0).astype(dtype)


def rounded(left, right):
    return dot(left, right).astype(jnp.bfloat16)


def begin_kernel(
    order, x_hbm, gain_hbm, first_hbm, second_hbm, gate_hbm, incoming_hbm, out_hbm,
    normed_ref, inv_ref, first_recv_ref, second_send_ref, second_recv_ref,
    mix_factor_ref, slope_ref, hidden_ref, keep_ref, give_ref,
    x_ref, gain_ref, first_ref, second_ref, gate_ref, incoming_ref, out_ref, sems,
):
    parts = chunks(out_hbm.shape[0], sems.shape[0] - 6)
    pairs = [(x_hbm, x_ref), (first_hbm, first_ref), (second_hbm, second_ref), (gain_hbm, gain_ref)]
    pairs += [(gate_hbm, gate_ref), (incoming_hbm, incoming_ref)]
    pairs += [(out_hbm.at[rows], out_ref.at[rows]) for rows in parts]
    copies = [pltpu.make_async_copy(*pair, sems.at[i]) for i, pair in enumerate(pairs)]
    for copy in copies[:5]:
        copy.start()
    active = lax.axis_index("pipe") == lax.axis_size("pipe") - 1

    @pl.when(active)
    def _():
        for copy in copies[5:]:
            copy.start()

    me = lax.axis_index("seq")
    down, across = positions(order)
    for copy in copies[:4]:
        copy.wait()
    first = block_diagonal([first_ref[k].astype(jnp.float32) for k in range(order.local_blocks)])
    second = block_diagonal([second_ref[k].astype(jnp.float32) for k in range(order.local_blocks)])
    sent, received = order.sent(down), order.received(across)
    first_send = rounded(
        one_hot(order.first_rows(me, sent, down) == across), first.astype(jnp.bfloat16)
    )
    second_send_ref[...] = rounded(
        one_hot(order.second_rows(me, sent, down) == across), second.T.astype(jnp.bfloat16)
    )
    first_recv_ref[...] = rounded(
        first.T.astype(jnp.bfloat16), one_hot(order.first_rows(me, received, across) == down)
    )
    second_recv_ref[...] = rounded(
        second.astype(jnp.bfloat16), one_hot(order.second_rows(me, received, across) == down)
    )
    features = x_ref[...].astype(jnp.float32)
    inv_rms = lax.rsqrt(jnp.mean(features * features, axis=-1, keepdims=True) + 1e-06)
    inv_ref[...] = inv_rms
    normed = (features * inv_rms * gain_ref[...]).astype(jnp.bfloat16)
    normed_ref[...] = normed

    def place(send, stream, columns):
        for core, target in enumerate((keep_ref, give_ref)):
            for chip in range(order.chips):
                rows = order.rows(2 * chip + stream)
                target[rows, columns] = send[order.rows(core * order.chips + chip)]

    place(rounded(first_send, normed), 0, slice(None))
    copies[4].wait()
    gate_pre = dot(normed, gate_ref[...])
    sigma = jax.nn.sigmoid(gate_pre)
    mix_factor_ref[...] = gate_pre * sigma
    slope_ref[...] = sigma * (1.0 + gate_pre * (1.0 - sigma))

    @pl.when(active)
    def _():
        copies[5].wait()
        for columns, copy in zip(parts, copies[6:]):
            copy.wait()
            hidden = dot_rows(incoming_ref[...], out_ref[columns])
            hidden_ref[:, columns] = hidden
            mix = (hidden * mix_factor_ref[:, columns]).astype(jnp.bfloat16)
            place(rounded(second_send_ref[...], mix), 1, columns)

    @pl.when(jnp.logical_not(active))
    def _():
        hidden_ref[...] = jnp.zeros(hidden_ref.shape, hidden_ref.dtype)
        place(jnp.zeros(normed_ref.shape, normed_ref.dtype), 1, slice(None))


def begin(order, *operands):
    row_count, width = operands[0].shape
    square = array_of((row_count, row_count), jnp.bfloat16)
    short = array_of((row_count, width), jnp.bfloat16)
    full = array_of((row_count, width), jnp.float32)
    column = array_of((row_count, 1), jnp.float32)
    outs = [short, column, square, square, square, full, full, full, short, short]
    return pl.pallas_call(
        functools.partial(begin_kernel, order),
        in_specs=[ANYWHERE] * len(operands),
        out_specs=[WHOLE] * len(outs),
        out_shape=outs,
        scratch_shapes=[pltpu.VMEM(o.shape, o.dtype) for o in operands]
        + [pltpu.SemaphoreType.DMA((9,))],
        compiler_params=granted(13),
        name="begin",
    )(*[in_hbm(o) for o in operands])


def transpose_kernel(gate_hbm, out_hbm, after_ref, gate_turned_ref, *refs):
    out_turned_refs, (gate_held, out_held, sems) = refs[:-3], refs[-3:]
    parts = chunks(gate_held.shape[0], sems.shape[1])
    work = []
    for i, (source, held) in enumerate(((gate_hbm, gate_held), (out_hbm, out_held))):
        for j, rows in enumerate(parts):
            copy = pltpu.make_async_copy(source.at[rows], held.at[rows], sems.at[i, j])
            copy.start()
            work.append((copy, held, rows, [gate_turned_ref] if i == 0 else out_turned_refs))
    for copy, held, rows, targets in work:
        copy.wait()
        for target, columns in zip(targets, chunks(held.shape[1], len(targets))):
            target[:, rows] = held[rows, columns].T


def transposed(weight_gate, weight_out, after):
    height, width = weight_out.shape
    half = pltpu.VMEM((width // HALVES, height), jnp.bfloat16)
    return pl.pallas_call(
        transpose_kernel,
        in_specs=[ANYWHERE] * 3,
        out_specs=[WHOLE] * (1 + HALVES),
        out_shape=[pltpu.VMEM(weight_gate.shape[::-1], jnp.bfloat16)] + [half] * HALVES,
        scratch_shapes=[
            pltpu.VMEM(weight_gate.shape, weight_gate.dtype),
            pltpu.VMEM(weight_out.shape, weight_out.dtype),
            pltpu.SemaphoreType.DMA((2, 6)),
        ],
        compiler_params=granted(11),
        name="transposed",
    )(in_hbm(weight_gate), in_hbm(weight_out), after)


def joined(refs):
    return jnp.concatenate([ref[...] for ref in refs], axis=1)


def store_halves(refs, value):
    for ref, columns in zip(refs, chunks(value.shape[1], len(refs))):
        ref[...] = value[:, columns]


def outgoing_of(gate_back, first_back, gain, inputs, inv_rms, incoming):
    delta_norm = (first_back + gate_back) * gain
    unit_rows = inputs.astype(jnp.float32) * inv_rms
    centred = delta_norm - unit_rows * jnp.mean(delta_norm * unit_rows, axis=-1, keepdims=True)
    return (incoming.astype(jnp.float32) + inv_rms * centred).astype(jnp.bfloat16)


def finish_kernel(order, *refs):
    arrived, refs = refs[: order.chips], refs[order.chips :]
    (
        second_recv_ref, first_recv_ref, slope_ref, hidden_ref, gate_ref, gain_ref, x_ref, inv_ref,
        incoming_ref, moved_ref, mid_ref, gate_factor_ref, *outgoing_refs,
    ) = refs
    for chip, message in enumerate(arrived):
        for core in range(2):
            for stream, target in enumerate((moved_ref, mid_ref)):
                target[order.rows(2 * chip + core)] = message[order.rows(2 * core + stream)]
    gate_factor = dot(second_recv_ref[...], moved_ref[...]) * slope_ref[...]
    gate_factor_ref[...] = gate_factor
    delta_gate = (hidden_ref[...] * gate_factor).astype(jnp.bfloat16)
    gate_back = dot(delta_gate, gate_ref[...])
    first_back = dot(first_recv_ref[...], mid_ref[...])
    outgoing = outgoing_of(
        gate_back, first_back, gain_ref[...], x_ref[...], inv_ref[...], incoming_ref[...]
    )
    store_halves(outgoing_refs, outgoing)


def finish(order, *operands):
    row_count, width = operands[-1].shape
    short = array_of((row_count, width), jnp.bfloat16)
    full = array_of((row_count, width), jnp.float32)
    part = array_of((row_count, width // HALVES), jnp.bfloat16)
    return pl.pallas_call(
        functools.partial(finish_kernel, order),
        in_specs=[WHOLE] * len(operands),
        out_specs=[WHOLE] * (3 + HALVES),
        out_shape=[short, short, full] + [part] * HALVES,
        compiler_params=granted(4),
        name="finish",
    )(*operands)


def advance_kernel(
    after_ref, mid_ref, first_recv_ref, gate_back_ref, gain_ref, x_ref, inv_ref, *refs
):
    incoming_refs, outgoing_refs = refs[:HALVES], refs[HALVES:]
    first_back = dot(first_recv_ref[...], mid_ref[...])
    outgoing = outgoing_of(
        gate_back_ref[...], first_back, gain_ref[...], x_ref[...], inv_ref[...],
        joined(incoming_refs),
    )
    store_halves(outgoing_refs, outgoing)


def advance(incoming, *operands):
    return pl.pallas_call(
        advance_kernel,
        in_specs=[WHOLE] * (len(operands) + HALVES),
        out_specs=[WHOLE] * HALVES,
        out_shape=[array_of(part.shape, part.dtype) for part in incoming],
        compiler_params=granted(4),
        name="advance",
    )(*operands, *incoming)


def exact(left, right):
    return jnp.dot(
        left, right, precision=lax.Precision.HIGHEST, preferred_element_type=jnp.float32
    )


def keep_kernel(order, section, after_ref, normed_ref, moved_ref, mid_ref, mix_ref, *refs):
    outgoing_refs, kept, new = refs[:HALVES], refs[HALVES : HALVES + 3], refs[HALVES + 3 :]
    index = lax.axis_index("pipe")
    new[0][...] = jnp.where(index == section + 1, joined(outgoing_refs), kept[0][...])
    first = dot_rows(mid_ref[...], normed_ref[...])
    new[1][...] = jnp.where(index == section + 1, first, kept[1][...])
    second = dot_rows(mix_ref[...], moved_ref[...])
    second = jnp.where(index == section, second, kept[2][...])
    if section > 0:
        new[2][...] = second
        return
    down, across = positions(order)
    rows_of = order.second_rows(lax.axis_index("seq"), order.received(down), down)
    second = exact(second, one_hot(rows_of == across, jnp.float32))
    for k, rows in enumerate(chunks(order.row_count, order.local_blocks)):
        new[2][k] = second[rows, rows]


def keep_first_kernel(
    order, section, after_ref, normed_ref, moved_ref, mid_ref, mix_ref, hidden_ref, mix_factor_ref, *refs
):
    outgoing_refs, new = refs[:HALVES], refs[HALVES:]
    new[0][...] = joined(outgoing_refs)
    new[1][...] = dot_rows(mid_ref[...], normed_ref[...])
    before = (hidden_ref[...] * mix_factor_ref[...]).astype(jnp.bfloat16)
    mix = jnp.where(lax.axis_index("pipe") == section, mix_ref[...], before)
    new[2][...] = dot_rows(mix, moved_ref[...])


def close_kernel(
    order, mid_ref, first_recv_ref, gate_back_ref, gain_ref, x_ref, inv_ref, normed_ref, *refs
):
    incoming_refs, refs = refs[:HALVES], refs[HALVES:]
    outgoing_kept_ref, first_kept_ref, outgoing_ref, first_ref = refs
    active = lax.axis_index("pipe") == 0
    first_back = dot(first_recv_ref[...], mid_ref[...])
    outgoing = outgoing_of(
        gate_back_ref[...], first_back, gain_ref[...], x_ref[...], inv_ref[...],
        joined(incoming_refs),
    )
    outgoing_ref[...] = jnp.where(active, outgoing, outgoing_kept_ref[...])
    first = jnp.where(active, dot_rows(mid_ref[...], normed_ref[...]), first_kept_ref[...])
    down, across = positions(order)
    rows_of = order.first_rows(lax.axis_index("seq"), order.received(across), across)
    first = exact(one_hot(rows_of == down, jnp.float32), first)
    for k, rows in enumerate(chunks(order.row_count, order.local_blocks)):
        first_ref[k] = first[rows, rows]


def call(kernel, name, outs, operands):
    return pl.pallas_call(
        kernel,
        in_specs=[WHOLE] * len(operands),
        out_specs=[WHOLE] * len(outs),
        out_shape=outs,
        compiler_params=granted(4),
        name=name,
    )(*operands)


def per_device(section_inputs, cotangent, gain, w_gate, w_out, mix_first, mix_second):
    inputs = section_inputs[0]
    local_blocks, block_rows = mix_first.shape[1:3]
    section_count = lax.axis_size("pipe")
    order = Order(inputs.shape[0], local_blocks, block_rows, lax.axis_size("seq"))

    (
        normed, inv_rms, first_recv, second_send, second_recv,
        mix_factor, slope, delta_hidden, kept, give,
    ) = begin(
        order, inputs, gain, mix_first[0], mix_second[0], w_gate[0], cotangent, w_out[0]
    )
    arrived = order.exchange(kept, give, streams=2)
    gate_turned, *out_turned = transposed(w_gate[0], w_out[0], arrived[0])
    moved, delta_mid, gate_factor, *outgoing = finish(
        order, *arrived, second_recv, first_recv, slope, delta_hidden, gate_turned, gain,
        inputs, inv_rms, cotangent,
    )

    row_count, width = inputs.shape
    short = array_of((row_count, width), jnp.bfloat16)
    square = array_of((row_count, row_count), jnp.float32)
    blocks = array_of((local_blocks, block_rows, block_rows), jnp.float32)
    kept = (delta_hidden, mix_factor)
    for sender in reversed(range(section_count - 1)):
        before = (delta_mid, *outgoing)
        incoming = [passed_down(part, sender + 1) for part in outgoing]
        delta_hidden = sum(dot(part, weight) for part, weight in zip(incoming, out_turned))
        delta_mix = (delta_hidden * mix_factor).astype(jnp.bfloat16)
        send = rounded(second_send, delta_mix)
        arrived = order.exchange(*jnp.split(send, 2))
        before_mid, *before_outgoing = before
        if sender + 2 == section_count:
            kept = call(
                functools.partial(keep_first_kernel, order, sender), "keep", [short, square, square],
                (arrived[0], normed, moved, before_mid, delta_mix, *kept, *before_outgoing),
            )
        else:
            kept = call(
                functools.partial(keep_kernel, order, sender), "keep",
                [short, square, square if sender else blocks],
                (arrived[0], normed, moved, before_mid, delta_mix, *before_outgoing, *kept),
            )
        delta_mid = jnp.concatenate(arrived)
        delta_gate = (delta_hidden * gate_factor).astype(jnp.bfloat16)
        gate_back = dot(delta_gate, gate_turned)
        if sender > 0:
            outgoing = advance(incoming, kept[1], delta_mid, first_recv, gate_back, gain, inputs, inv_rms)
    outgoing_kept, first_kept, grad_second = kept
    grad_inputs, grad_first = call(
        functools.partial(close_kernel, order), "close", [short, blocks],
        (
            delta_mid, first_recv, gate_back, gain, inputs, inv_rms, normed, *incoming,
            outgoing_kept, first_kept,
        ),
    )
    return (grad_inputs[None], grad_first[None], grad_second[None])


def solution(mesh):
    placed = (
        P("pipe", "seq", None),
        P("seq", None),
        P("pipe", None),
        P("pipe", None, None),
        P("pipe", None, None),
        P("pipe", "seq", None, None),
        P("pipe", "seq", None, None),
    )
    return jax.shard_map(
        per_device,
        mesh=mesh,
        in_specs=placed,
        out_specs=(
            P("pipe", "seq", None),
            P("pipe", "seq", None, None),
            P("pipe", "seq", None, None),
        ),
        check_vma=False,
    )
```

```python
import functools

import jax
import jax.numpy as jnp
from jax import lax
from jax.experimental import pallas as pl
from jax.experimental.pallas import tpu as pltpu
from jax.sharding import PartitionSpec as P

ROWS_BY_ROWS = (((1,), (1,)), ((), ()))
WHOLE = pl.BlockSpec(memory_space=pltpu.VMEM)
ANYWHERE = pl.BlockSpec(memory_space=pl.ANY)
HALVES = 2


def granted(mebibytes):
    return pltpu.CompilerParams(vmem_limit_bytes=mebibytes << 20)


def in_hbm(array):
    return pltpu.with_memory_space_constraint(array, pltpu.HBM)


def array_of(shape, dtype):
    return jax.ShapeDtypeStruct(shape, dtype)


def dot(left, right):
    return jnp.dot(left, right, preferred_element_type=jnp.float32)


def dot_rows(left, right):
    return lax.dot_general(left, right, ROWS_BY_ROWS, preferred_element_type=jnp.float32)


def swap(block, offset):
    count = lax.axis_size("seq")
    return lax.ppermute(block, "seq", [(i, i ^ offset) for i in range(count)])


def passed_down(block, sender):
    sections = lax.axis_size("pipe")
    pairs = []
    for device in range(lax.axis_size("seq")):
        for section in range(sections):
            target = (device ^ 1, section)
            if section in (sender, sender - 1):
                target = (device, 2 * sender - 1 - section)
            pairs.append((device * sections + section, target[0] * sections + target[1]))
    return lax.ppermute(block, ("seq", "pipe"), pairs)


def chunks(size, count):
    return [slice(i * size // count, (i + 1) * size // count) for i in range(count)]


def log2(size):
    assert size & (size - 1) == 0
    return size.bit_length() - 1


class Order:
    def __init__(self, row_count, local_blocks, block_rows, seq_count):
        self.row_count = row_count
        self.local_blocks = local_blocks
        self.block_rows = block_rows
        self.seq_count = seq_count
        self.chips = seq_count // 2
        self.steps = block_rows // seq_count
        self.piece = local_blocks * self.steps

    def rows(self, group, count=1):
        return slice(group * self.piece, (group + count) * self.piece)

    def sent(self, position):
        group = position >> log2(self.piece)
        return (group >> log2(self.chips)) + 2 * (group & (self.chips - 1))

    def received(self, position):
        return position >> log2(self.piece)

    def first_rows(self, me, partner, position):
        block = (position >> log2(self.steps)) & (self.local_blocks - 1)
        step = position & (self.steps - 1)
        return block * self.block_rows + (me ^ partner) * self.steps + step

    def second_rows(self, me, partner, position):
        block = (position >> log2(self.steps)) & (self.local_blocks - 1)
        step = position & (self.steps - 1)
        return (step * self.seq_count + (me ^ partner)) * self.local_blocks + block

    def exchange(self, kept, give, streams=1):
        got = swap(give, 1)
        arrived = []
        for chip in range(self.chips):
            rows = self.rows(chip * streams, streams)
            message = jnp.concatenate([kept[rows], got[rows]])
            arrived.append(swap(message, 2 * chip) if chip else message)
        return arrived


def block_diagonal(blocks):
    zero = jnp.zeros(blocks[0].shape, blocks[0].dtype)
    return jnp.concatenate(
        [
            jnp.concatenate([b if k == j else zero for j in range(len(blocks))], axis=1)
            for k, b in enumerate(blocks)
        ],
        axis=0,
    )


def positions(order):
    square = (order.row_count, order.row_count)
    return lax.broadcasted_iota(jnp.int32, square, 0), lax.broadcasted_iota(jnp.int32, square, 1)


def one_hot(matches, dtype=jnp.bfloat16):
    return jnp.where(matches, 1.0, 0.0).astype(dtype)


def rounded(left, right):
    return dot(left, right).astype(jnp.bfloat16)


def begin_kernel(
    order, x_hbm, gain_hbm, first_hbm, second_hbm, gate_hbm, incoming_hbm, out_hbm,
    normed_ref, inv_ref, first_recv_ref, second_send_ref, second_recv_ref,
    mix_factor_ref, slope_ref, hidden_ref, keep_ref, give_ref,
    x_ref, gain_ref, first_ref, second_ref, gate_ref, incoming_ref, out_ref, sems,
):
    parts = chunks(out_hbm.shape[0], sems.shape[0] - 6)
    pairs = [(x_hbm, x_ref), (first_hbm, first_ref), (second_hbm, second_ref), (gain_hbm, gain_ref)]
    pairs += [(gate_hbm, gate_ref), (incoming_hbm, incoming_ref)]
    pairs += [(out_hbm.at[rows], out_ref.at[rows]) for rows in parts]
    copies = [pltpu.make_async_copy(*pair, sems.at[i]) for i, pair in enumerate(pairs)]
    for copy in copies[:5]:
        copy.start()
    active = lax.axis_index("pipe") == lax.axis_size("pipe") - 1

    @pl.when(active)
    def _():
        for copy in copies[5:]:
            copy.start()

    me = lax.axis_index("seq")
    down, across = positions(order)
    for copy in copies[:4]:
        copy.wait()
    first = block_diagonal([first_ref[k].astype(jnp.float32) for k in range(order.local_blocks)])
    second = block_diagonal([second_ref[k].astype(jnp.float32) for k in range(order.local_blocks)])
    sent, received = order.sent(down), order.received(across)
    first_send = rounded(
        one_hot(order.first_rows(me, sent, down) == across), first.astype(jnp.bfloat16)
    )
    second_send_ref[...] = rounded(
        one_hot(order.second_rows(me, sent, down) == across), second.T.astype(jnp.bfloat16)
    )
    first_recv_ref[...] = rounded(
        first.T.astype(jnp.bfloat16), one_hot(order.first_rows(me, received, across) == down)
    )
    second_recv_ref[...] = rounded(
        second.astype(jnp.bfloat16), one_hot(order.second_rows(me, received, across) == down)
    )
    features = x_ref[...].astype(jnp.float32)
    inv_rms = lax.rsqrt(jnp.mean(features * features, axis=-1, keepdims=True) + 1e-06)
    inv_ref[...] = inv_rms
    normed = (features * inv_rms * gain_ref[...]).astype(jnp.bfloat16)
    normed_ref[...] = normed

    def place(send, stream, columns):
        for core, target in enumerate((keep_ref, give_ref)):
            for chip in range(order.chips):
                rows = order.rows(2 * chip + stream)
                target[rows, columns] = send[order.rows(core * order.chips + chip)]

    place(rounded(first_send, normed), 0, slice(None))
    copies[4].wait()
    gate_pre = dot(normed, gate_ref[...])
    sigma = jax.nn.sigmoid(gate_pre)
    mix_factor_ref[...] = gate_pre * sigma
    slope_ref[...] = sigma * (1.0 + gate_pre * (1.0 - sigma))

    @pl.when(active)
    def _():
        copies[5].wait()
        for columns, copy in zip(parts, copies[6:]):
            copy.wait()
            hidden = dot_rows(incoming_ref[...], out_ref[columns])
            hidden_ref[:, columns] = hidden
            mix = (hidden * mix_factor_ref[:, columns]).astype(jnp.bfloat16)
            place(rounded(second_send_ref[...], mix), 1, columns)

    @pl.when(jnp.logical_not(active))
    def _():
        hidden_ref[...] = jnp.zeros(hidden_ref.shape, hidden_ref.dtype)
        place(jnp.zeros(normed_ref.shape, normed_ref.dtype), 1, slice(None))


def begin(order, *operands):
    row_count, width = operands[0].shape
    square = array_of((row_count, row_count), jnp.bfloat16)
    short = array_of((row_count, width), jnp.bfloat16)
    full = array_of((row_count, width), jnp.float32)
    column = array_of((row_count, 1), jnp.float32)
    outs = [short, column, square, square, square, full, full, full, short, short]
    return pl.pallas_call(
        functools.partial(begin_kernel, order),
        in_specs=[ANYWHERE] * len(operands),
        out_specs=[WHOLE] * len(outs),
        out_shape=outs,
        scratch_shapes=[pltpu.VMEM(o.shape, o.dtype) for o in operands]
        + [pltpu.SemaphoreType.DMA((9,))],
        compiler_params=granted(13),
        name="begin",
    )(*[in_hbm(o) for o in operands])


def transpose_kernel(gate_hbm, out_hbm, after_ref, gate_turned_ref, *refs):
    out_turned_refs, (gate_held, out_held, sems) = refs[:-3], refs[-3:]
    parts = chunks(gate_held.shape[0], sems.shape[1])
    work = []
    for i, (source, held) in enumerate(((gate_hbm, gate_held), (out_hbm, out_held))):
        for j, rows in enumerate(parts):
            copy = pltpu.make_async_copy(source.at[rows], held.at[rows], sems.at[i, j])
            copy.start()
            work.append((copy, held, rows, [gate_turned_ref] if i == 0 else out_turned_refs))
    for copy, held, rows, targets in work:
        copy.wait()
        for target, columns in zip(targets, chunks(held.shape[1], len(targets))):
            target[:, rows] = held[rows, columns].T


def transposed(weight_gate, weight_out, after):
    height, width = weight_out.shape
    half = pltpu.VMEM((width // HALVES, height), jnp.bfloat16)
    return pl.pallas_call(
        transpose_kernel,
        in_specs=[ANYWHERE] * 3,
        out_specs=[WHOLE] * (1 + HALVES),
        out_shape=[pltpu.VMEM(weight_gate.shape[::-1], jnp.bfloat16)] + [half] * HALVES,
        scratch_shapes=[
            pltpu.VMEM(weight_gate.shape, weight_gate.dtype),
            pltpu.VMEM(weight_out.shape, weight_out.dtype),
            pltpu.SemaphoreType.DMA((2, 6)),
        ],
        compiler_params=granted(11),
        name="transposed",
    )(in_hbm(weight_gate), in_hbm(weight_out), after)


def joined(refs):
    return jnp.concatenate([ref[...] for ref in refs], axis=1)


def store_halves(refs, value):
    for ref, columns in zip(refs, chunks(value.shape[1], len(refs))):
        ref[...] = value[:, columns]


def outgoing_of(gate_back, first_back, gain, inputs, inv_rms, incoming):
    delta_norm = (first_back + gate_back) * gain
    unit_rows = inputs.astype(jnp.float32) * inv_rms
    centred = delta_norm - unit_rows * jnp.mean(delta_norm * unit_rows, axis=-1, keepdims=True)
    return (incoming.astype(jnp.float32) + inv_rms * centred).astype(jnp.bfloat16)


def finish_kernel(order, *refs):
    arrived, refs = refs[: order.chips], refs[order.chips :]
    (
        second_recv_ref, first_recv_ref, slope_ref, hidden_ref, gate_ref, gain_ref, x_ref, inv_ref,
        incoming_ref, moved_ref, mid_ref, gate_factor_ref, *outgoing_refs,
    ) = refs
    for chip, message in enumerate(arrived):
        for core in range(2):
            for stream, target in enumerate((moved_ref, mid_ref)):
                target[order.rows(2 * chip + core)] = message[order.rows(2 * core + stream)]
    gate_factor = dot(second_recv_ref[...], moved_ref[...]) * slope_ref[...]
    gate_factor_ref[...] = gate_factor
    delta_gate = (hidden_ref[...] * gate_factor).astype(jnp.bfloat16)
    gate_back = dot(delta_gate, gate_ref[...])
    first_back = dot(first_recv_ref[...], mid_ref[...])
    outgoing = outgoing_of(
        gate_back, first_back, gain_ref[...], x_ref[...], inv_ref[...], incoming_ref[...]
    )
    store_halves(outgoing_refs, outgoing)


def finish(order, *operands):
    row_count, width = operands[-1].shape
    short = array_of((row_count, width), jnp.bfloat16)
    full = array_of((row_count, width), jnp.float32)
    part = array_of((row_count, width // HALVES), jnp.bfloat16)
    return pl.pallas_call(
        functools.partial(finish_kernel, order),
        in_specs=[WHOLE] * len(operands),
        out_specs=[WHOLE] * (3 + HALVES),
        out_shape=[short, short, full] + [part] * HALVES,
        compiler_params=granted(4),
        name="finish",
    )(*operands)


def advance_kernel(
    after_ref, mid_ref, first_recv_ref, gate_back_ref, gain_ref, x_ref, inv_ref, *refs
):
    incoming_refs, outgoing_refs = refs[:HALVES], refs[HALVES:]
    first_back = dot(first_recv_ref[...], mid_ref[...])
    outgoing = outgoing_of(
        gate_back_ref[...], first_back, gain_ref[...], x_ref[...], inv_ref[...],
        joined(incoming_refs),
    )
    store_halves(outgoing_refs, outgoing)


def advance(incoming, *operands):
    return pl.pallas_call(
        advance_kernel,
        in_specs=[WHOLE] * (len(operands) + HALVES),
        out_specs=[WHOLE] * HALVES,
        out_shape=[array_of(part.shape, part.dtype) for part in incoming],
        compiler_params=granted(4),
        name="advance",
    )(*operands, *incoming)


def exact(left, right):
    return jnp.dot(
        left, right, precision=lax.Precision.HIGHEST, preferred_element_type=jnp.float32
    )


def keep_kernel(order, section, after_ref, normed_ref, moved_ref, mid_ref, mix_ref, *refs):
    outgoing_refs, kept, new = refs[:HALVES], refs[HALVES : HALVES + 3], refs[HALVES + 3 :]
    index = lax.axis_index("pipe")
    new[0][...] = jnp.where(index == section + 1, joined(outgoing_refs), kept[0][...])
    first = dot_rows(mid_ref[...], normed_ref[...])
    new[1][...] = jnp.where(index == section + 1, first, kept[1][...])
    second = dot_rows(mix_ref[...], moved_ref[...])
    second = jnp.where(index == section, second, kept[2][...])
    if section > 0:
        new[2][...] = second
        return
    down, across = positions(order)
    rows_of = order.second_rows(lax.axis_index("seq"), order.received(down), down)
    second = exact(second, one_hot(rows_of == across, jnp.float32))
    for k, rows in enumerate(chunks(order.row_count, order.local_blocks)):
        new[2][k] = second[rows, rows]


def keep_first_kernel(
    order, section, after_ref, normed_ref, moved_ref, mid_ref, mix_ref, hidden_ref, mix_factor_ref, *refs
):
    outgoing_refs, new = refs[:HALVES], refs[HALVES:]
    new[0][...] = joined(outgoing_refs)
    new[1][...] = dot_rows(mid_ref[...], normed_ref[...])
    before = (hidden_ref[...] * mix_factor_ref[...]).astype(jnp.bfloat16)
    mix = jnp.where(lax.axis_index("pipe") == section, mix_ref[...], before)
    new[2][...] = dot_rows(mix, moved_ref[...])


def close_kernel(
    order, mid_ref, first_recv_ref, gate_back_ref, gain_ref, x_ref, inv_ref, normed_ref, *refs
):
    incoming_refs, refs = refs[:HALVES], refs[HALVES:]
    outgoing_kept_ref, first_kept_ref, outgoing_ref, first_ref = refs
    active = lax.axis_index("pipe") == 0
    first_back = dot(first_recv_ref[...], mid_ref[...])
    outgoing = outgoing_of(
        gate_back_ref[...], first_back, gain_ref[...], x_ref[...], inv_ref[...],
        joined(incoming_refs),
    )
    outgoing_ref[...] = jnp.where(active, outgoing, outgoing_kept_ref[...])
    first = jnp.where(active, dot_rows(mid_ref[...], normed_ref[...]), first_kept_ref[...])
    down, across = positions(order)
    rows_of = order.first_rows(lax.axis_index("seq"), order.received(across), across)
    first = exact(one_hot(rows_of == down, jnp.float32), first)
    for k, rows in enumerate(chunks(order.row_count, order.local_blocks)):
        first_ref[k] = first[rows, rows]


def call(kernel, name, outs, operands):
    return pl.pallas_call(
        kernel,
        in_specs=[WHOLE] * len(operands),
        out_specs=[WHOLE] * len(outs),
        out_shape=outs,
        compiler_params=granted(4),
        name=name,
    )(*operands)


def per_device(section_inputs, cotangent, gain, w_gate, w_out, mix_first, mix_second):
    inputs = section_inputs[0]
    local_blocks, block_rows = mix_first.shape[1:3]
    section_count = lax.axis_size("pipe")
    order = Order(inputs.shape[0], local_blocks, block_rows, lax.axis_size("seq"))

    (
        normed, inv_rms, first_recv, second_send, second_recv,
        mix_factor, slope, delta_hidden, kept, give,
    ) = begin(
        order, inputs, gain, mix_first[0], mix_second[0], w_gate[0], cotangent, w_out[0]
    )
    arrived = order.exchange(kept, give, streams=2)
    gate_turned, *out_turned = transposed(w_gate[0], w_out[0], arrived[0])
    moved, delta_mid, gate_factor, *outgoing = finish(
        order, *arrived, second_recv, first_recv, slope, delta_hidden, gate_turned, gain,
        inputs, inv_rms, cotangent,
    )

    row_count, width = inputs.shape
    short = array_of((row_count, width), jnp.bfloat16)
    square = array_of((row_count, row_count), jnp.float32)
    blocks = array_of((local_blocks, block_rows, block_rows), jnp.float32)
    kept = (delta_hidden, mix_factor)
    for sender in reversed(range(section_count - 1)):
        before = (delta_mid, *outgoing)
        incoming = [passed_down(part, sender + 1) for part in outgoing]
        delta_hidden = sum(dot(part, weight) for part, weight in zip(incoming, out_turned))
        delta_mix = (delta_hidden * mix_factor).astype(jnp.bfloat16)
        send = rounded(second_send, delta_mix)
        arrived = order.exchange(*jnp.split(send, 2))
        before_mid, *before_outgoing = before
        if sender + 2 == section_count:
            kept = call(
                functools.partial(keep_first_kernel, order, sender), "keep", [short, square, square],
                (arrived[0], normed, moved, before_mid, delta_mix, *kept, *before_outgoing),
            )
        else:
            kept = call(
                functools.partial(keep_kernel, order, sender), "keep",
                [short, square, square if sender else blocks],
                (arrived[0], normed, moved, before_mid, delta_mix, *before_outgoing, *kept),
            )
        delta_mid = jnp.concatenate(arrived)
        delta_gate = (delta_hidden * gate_factor).astype(jnp.bfloat16)
        gate_back = dot(delta_gate, gate_turned)
        if sender > 0:
            outgoing = advance(incoming, kept[1], delta_mid, first_recv, gate_back, gain, inputs, inv_rms)
    outgoing_kept, first_kept, grad_second = kept
    grad_inputs, grad_first = call(
        functools.partial(close_kernel, order), "close", [short, blocks],
        (
            delta_mid, first_recv, gate_back, gain, inputs, inv_rms, normed, *incoming,
            outgoing_kept, first_kept,
        ),
    )
    return (grad_inputs[None], grad_first[None], grad_second[None])


def solution(mesh):
    placed = (
        P("pipe", "seq", None),
        P("seq", None),
        P("pipe", None),
        P("pipe", None, None),
        P("pipe", None, None),
        P("pipe", "seq", None, None),
        P("pipe", "seq", None, None),
    )
    return jax.shard_map(
        per_device,
        mesh=mesh,
        in_specs=placed,
        out_specs=(
            P("pipe", "seq", None),
            P("pipe", "seq", None, None),
            P("pipe", "seq", None, None),
        ),
        check_vma=False,
    )
```

```python
import functools

import jax
import jax.numpy as jnp
from jax import lax
from jax.experimental import pallas as pl
from jax.experimental.pallas import tpu as pltpu
from jax.sharding import PartitionSpec as P

ROWS_BY_ROWS = (((1,), (1,)), ((), ()))
WHOLE = pl.BlockSpec(memory_space=pltpu.VMEM)
ANYWHERE = pl.BlockSpec(memory_space=pl.ANY)
HALVES = 2


def granted(mebibytes):
    return pltpu.CompilerParams(vmem_limit_bytes=mebibytes << 20)


def in_hbm(array):
    return pltpu.with_memory_space_constraint(array, pltpu.HBM)


def array_of(shape, dtype):
    return jax.ShapeDtypeStruct(shape, dtype)


def dot(left, right):
    return jnp.dot(left, right, preferred_element_type=jnp.float32)


def dot_rows(left, right):
    return lax.dot_general(left, right, ROWS_BY_ROWS, preferred_element_type=jnp.float32)


def swap(block, offset):
    count = lax.axis_size("seq")
    return lax.ppermute(block, "seq", [(i, i ^ offset) for i in range(count)])


def passed_down(block, sender):
    sections = lax.axis_size("pipe")
    pairs = []
    for device in range(lax.axis_size("seq")):
        for section in range(sections):
            target = (device ^ 1, section)
            if section in (sender, sender - 1):
                target = (device, 2 * sender - 1 - section)
            pairs.append((device * sections + section, target[0] * sections + target[1]))
    return lax.ppermute(block, ("seq", "pipe"), pairs)


def chunks(size, count):
    return [slice(i * size // count, (i + 1) * size // count) for i in range(count)]


def column_parts(width):
    cut = width // 3 // 128 * 128
    return [slice(0, cut), slice(cut, width)]


def log2(size):
    assert size & (size - 1) == 0
    return size.bit_length() - 1


class Order:
    def __init__(self, row_count, local_blocks, block_rows, seq_count):
        self.row_count = row_count
        self.local_blocks = local_blocks
        self.block_rows = block_rows
        self.seq_count = seq_count
        self.chips = seq_count // 2
        self.steps = block_rows // seq_count
        self.piece = local_blocks * self.steps

    def rows(self, group, count=1):
        return slice(group * self.piece, (group + count) * self.piece)

    def sent(self, position):
        group = position >> log2(self.piece)
        return (group >> log2(self.chips)) + 2 * (group & (self.chips - 1))

    def received(self, position):
        return position >> log2(self.piece)

    def first_rows(self, me, partner, position):
        block = (position >> log2(self.steps)) & (self.local_blocks - 1)
        step = position & (self.steps - 1)
        return block * self.block_rows + (me ^ partner) * self.steps + step

    def second_rows(self, me, partner, position):
        block = (position >> log2(self.steps)) & (self.local_blocks - 1)
        step = position & (self.steps - 1)
        return (step * self.seq_count + (me ^ partner)) * self.local_blocks + block

    def exchange(self, kept, give, streams=1):
        got = swap(give, 1)
        arrived = []
        for chip in range(self.chips):
            rows = self.rows(chip * streams, streams)
            message = jnp.concatenate([kept[rows], got[rows]])
            arrived.append(swap(message, 2 * chip) if chip else message)
        return arrived


def block_diagonal(blocks):
    zero = jnp.zeros(blocks[0].shape, blocks[0].dtype)
    return jnp.concatenate(
        [
            jnp.concatenate([b if k == j else zero for j in range(len(blocks))], axis=1)
            for k, b in enumerate(blocks)
        ],
        axis=0,
    )


def positions(order):
    square = (order.row_count, order.row_count)
    return lax.broadcasted_iota(jnp.int32, square, 0), lax.broadcasted_iota(jnp.int32, square, 1)


def one_hot(matches, dtype=jnp.bfloat16):
    return jnp.where(matches, 1.0, 0.0).astype(dtype)


def rounded(left, right):
    return dot(left, right).astype(jnp.bfloat16)


def begin_kernel(
    order, x_hbm, gain_hbm, first_hbm, second_hbm, gate_hbm, incoming_hbm, out_hbm,
    normed_ref, inv_ref, first_recv_ref, second_send_ref, second_recv_ref,
    mix_factor_ref, slope_ref, hidden_ref, keep_ref, give_ref,
    x_ref, gain_ref, first_ref, second_ref, gate_ref, incoming_ref, out_ref, sems,
):
    parts = chunks(out_hbm.shape[0], sems.shape[0] - 6)
    pairs = [(x_hbm, x_ref), (first_hbm, first_ref), (second_hbm, second_ref), (gain_hbm, gain_ref)]
    pairs += [(gate_hbm, gate_ref), (incoming_hbm, incoming_ref)]
    pairs += [(out_hbm.at[rows], out_ref.at[rows]) for rows in parts]
    copies = [pltpu.make_async_copy(*pair, sems.at[i]) for i, pair in enumerate(pairs)]
    for copy in copies[:5]:
        copy.start()
    active = lax.axis_index("pipe") == lax.axis_size("pipe") - 1

    @pl.when(active)
    def _():
        for copy in copies[5:]:
            copy.start()

    me = lax.axis_index("seq")
    down, across = positions(order)
    for copy in copies[:4]:
        copy.wait()
    first = block_diagonal([first_ref[k].astype(jnp.float32) for k in range(order.local_blocks)])
    second = block_diagonal([second_ref[k].astype(jnp.float32) for k in range(order.local_blocks)])
    sent, received = order.sent(down), order.received(across)
    first_send = rounded(
        one_hot(order.first_rows(me, sent, down) == across), first.astype(jnp.bfloat16)
    )
    second_send_ref[...] = rounded(
        one_hot(order.second_rows(me, sent, down) == across), second.T.astype(jnp.bfloat16)
    )
    first_recv_ref[...] = rounded(
        first.T.astype(jnp.bfloat16), one_hot(order.first_rows(me, received, across) == down)
    )
    second_recv_ref[...] = rounded(
        second.astype(jnp.bfloat16), one_hot(order.second_rows(me, received, across) == down)
    )
    features = x_ref[...].astype(jnp.float32)
    inv_rms = lax.rsqrt(jnp.mean(features * features, axis=-1, keepdims=True) + 1e-06)
    inv_ref[...] = inv_rms
    normed = (features * inv_rms * gain_ref[...]).astype(jnp.bfloat16)
    normed_ref[...] = normed

    def place(send, stream, columns):
        for core, target in enumerate((keep_ref, give_ref)):
            for chip in range(order.chips):
                rows = order.rows(2 * chip + stream)
                target[rows, columns] = send[order.rows(core * order.chips + chip)]

    place(rounded(first_send, normed), 0, slice(None))
    copies[4].wait()
    gate_pre = dot(normed, gate_ref[...])
    sigma = jax.nn.sigmoid(gate_pre)
    mix_factor_ref[...] = gate_pre * sigma
    slope_ref[...] = sigma * (1.0 + gate_pre * (1.0 - sigma))

    @pl.when(active)
    def _():
        copies[5].wait()
        for columns, copy in zip(parts, copies[6:]):
            copy.wait()
            hidden_ref[:, columns] = dot_rows(incoming_ref[...], out_ref[columns])
        mix = (hidden_ref[...] * mix_factor_ref[...]).astype(jnp.bfloat16)
        place(rounded(second_send_ref[...], mix), 1, slice(None))

    @pl.when(jnp.logical_not(active))
    def _():
        hidden_ref[...] = jnp.zeros(hidden_ref.shape, hidden_ref.dtype)
        place(jnp.zeros(normed_ref.shape, normed_ref.dtype), 1, slice(None))


def begin(order, *operands):
    row_count, width = operands[0].shape
    square = array_of((row_count, row_count), jnp.bfloat16)
    short = array_of((row_count, width), jnp.bfloat16)
    full = array_of((row_count, width), jnp.float32)
    column = array_of((row_count, 1), jnp.float32)
    outs = [short, column, square, square, square, full, full, full, short, short]
    return pl.pallas_call(
        functools.partial(begin_kernel, order),
        in_specs=[ANYWHERE] * len(operands),
        out_specs=[WHOLE] * len(outs),
        out_shape=outs,
        scratch_shapes=[pltpu.VMEM(o.shape, o.dtype) for o in operands]
        + [pltpu.SemaphoreType.DMA((9,))],
        compiler_params=granted(13),
        name="begin",
    )(*[in_hbm(o) for o in operands])


def transpose_kernel(gate_hbm, out_hbm, after_ref, gate_turned_ref, *refs):
    out_turned_refs, (gate_held, out_held, sems) = refs[:-3], refs[-3:]
    parts = chunks(gate_held.shape[0], sems.shape[1])
    work = []
    for i, (source, held) in enumerate(((gate_hbm, gate_held), (out_hbm, out_held))):
        for j, rows in enumerate(parts):
            copy = pltpu.make_async_copy(source.at[rows], held.at[rows], sems.at[i, j])
            copy.start()
            work.append((copy, held, rows, [gate_turned_ref] if i == 0 else out_turned_refs))
    for copy, held, rows, targets in work:
        copy.wait()
        width = held.shape[1]
        columns_of = column_parts(width) if len(targets) > 1 else [slice(0, width)]
        for target, columns in zip(targets, columns_of):
            target[:, rows] = held[rows, columns].T


def transposed(weight_gate, weight_out, after):
    height, width = weight_out.shape
    parts = [pltpu.VMEM((c.stop - c.start, height), jnp.bfloat16) for c in column_parts(width)]
    return pl.pallas_call(
        transpose_kernel,
        in_specs=[ANYWHERE] * 3,
        out_specs=[WHOLE] * (1 + HALVES),
        out_shape=[pltpu.VMEM(weight_gate.shape[::-1], jnp.bfloat16)] + parts,
        scratch_shapes=[
            pltpu.VMEM(weight_gate.shape, weight_gate.dtype),
            pltpu.VMEM(weight_out.shape, weight_out.dtype),
            pltpu.SemaphoreType.DMA((2, 6)),
        ],
        compiler_params=granted(11),
        name="transposed",
    )(in_hbm(weight_gate), in_hbm(weight_out), after)


def joined(refs):
    return jnp.concatenate([ref[...] for ref in refs], axis=1)


def store_halves(refs, value):
    for ref, columns in zip(refs, column_parts(value.shape[1])):
        ref[...] = value[:, columns]


def outgoing_of(gate_back, first_back, gain, inputs, inv_rms, incoming):
    delta_norm = (first_back + gate_back) * gain
    unit_rows = inputs.astype(jnp.float32) * inv_rms
    centred = delta_norm - unit_rows * jnp.mean(delta_norm * unit_rows, axis=-1, keepdims=True)
    return (incoming.astype(jnp.float32) + inv_rms * centred).astype(jnp.bfloat16)


def finish_kernel(order, *refs):
    arrived, refs = refs[: order.chips], refs[order.chips :]
    (
        second_recv_ref, first_recv_ref, slope_ref, hidden_ref, gate_ref, gain_ref, x_ref, inv_ref,
        incoming_ref, moved_ref, mid_ref, gate_factor_ref, *outgoing_refs,
    ) = refs
    for chip, message in enumerate(arrived):
        for core in range(2):
            for stream, target in enumerate((moved_ref, mid_ref)):
                target[order.rows(2 * chip + core)] = message[order.rows(2 * core + stream)]
    gate_factor = dot(second_recv_ref[...], moved_ref[...]) * slope_ref[...]
    gate_factor_ref[...] = gate_factor
    delta_gate = (hidden_ref[...] * gate_factor).astype(jnp.bfloat16)
    gate_back = dot(delta_gate, gate_ref[...])
    first_back = dot(first_recv_ref[...], mid_ref[...])
    outgoing = outgoing_of(
        gate_back, first_back, gain_ref[...], x_ref[...], inv_ref[...], incoming_ref[...]
    )
    store_halves(outgoing_refs, outgoing)


def finish(order, *operands):
    row_count, width = operands[-1].shape
    short = array_of((row_count, width), jnp.bfloat16)
    full = array_of((row_count, width), jnp.float32)
    parts = [array_of((row_count, c.stop - c.start), jnp.bfloat16) for c in column_parts(width)]
    return pl.pallas_call(
        functools.partial(finish_kernel, order),
        in_specs=[WHOLE] * len(operands),
        out_specs=[WHOLE] * (3 + HALVES),
        out_shape=[short, short, full] + parts,
        compiler_params=granted(4),
        name="finish",
    )(*operands)


def advance_kernel(
    after_ref, mid_ref, first_recv_ref, gate_back_ref, gain_ref, x_ref, inv_ref, *refs
):
    incoming_refs, outgoing_refs = refs[:HALVES], refs[HALVES:]
    first_back = dot(first_recv_ref[...], mid_ref[...])
    outgoing = outgoing_of(
        gate_back_ref[...], first_back, gain_ref[...], x_ref[...], inv_ref[...],
        joined(incoming_refs),
    )
    store_halves(outgoing_refs, outgoing)


def advance(incoming, *operands):
    return pl.pallas_call(
        advance_kernel,
        in_specs=[WHOLE] * (len(operands) + HALVES),
        out_specs=[WHOLE] * HALVES,
        out_shape=[array_of(part.shape, part.dtype) for part in incoming],
        compiler_params=granted(4),
        name="advance",
    )(*operands, *incoming)


def exact(left, right):
    return jnp.dot(
        left, right, precision=lax.Precision.HIGHEST, preferred_element_type=jnp.float32
    )


def keep_kernel(order, section, after_ref, normed_ref, moved_ref, mid_ref, mix_ref, *refs):
    outgoing_refs, kept, new = refs[:HALVES], refs[HALVES : HALVES + 3], refs[HALVES + 3 :]
    index = lax.axis_index("pipe")
    new[0][...] = jnp.where(index == section + 1, joined(outgoing_refs), kept[0][...])
    first = dot_rows(mid_ref[...], normed_ref[...])
    new[1][...] = jnp.where(index == section + 1, first, kept[1][...])
    second = dot_rows(mix_ref[...], moved_ref[...])
    second = jnp.where(index == section, second, kept[2][...])
    if section > 0:
        new[2][...] = second
        return
    down, across = positions(order)
    rows_of = order.second_rows(lax.axis_index("seq"), order.received(down), down)
    second = exact(second, one_hot(rows_of == across, jnp.float32))
    for k, rows in enumerate(chunks(order.row_count, order.local_blocks)):
        new[2][k] = second[rows, rows]


def keep_first_kernel(
    order, section, after_ref, normed_ref, moved_ref, mid_ref, mix_ref, hidden_ref, mix_factor_ref, *refs
):
    outgoing_refs, new = refs[:HALVES], refs[HALVES:]
    new[0][...] = joined(outgoing_refs)
    new[1][...] = dot_rows(mid_ref[...], normed_ref[...])
    before = (hidden_ref[...] * mix_factor_ref[...]).astype(jnp.bfloat16)
    mix = jnp.where(lax.axis_index("pipe") == section, mix_ref[...], before)
    new[2][...] = dot_rows(mix, moved_ref[...])


def close_kernel(
    order, mid_ref, first_recv_ref, gate_back_ref, gain_ref, x_ref, inv_ref, normed_ref, *refs
):
    incoming_refs, refs = refs[:HALVES], refs[HALVES:]
    outgoing_kept_ref, first_kept_ref, outgoing_ref, first_ref = refs
    active = lax.axis_index("pipe") == 0
    first_back = dot(first_recv_ref[...], mid_ref[...])
    outgoing = outgoing_of(
        gate_back_ref[...], first_back, gain_ref[...], x_ref[...], inv_ref[...],
        joined(incoming_refs),
    )
    outgoing_ref[...] = jnp.where(active, outgoing, outgoing_kept_ref[...])
    first = jnp.where(active, dot_rows(mid_ref[...], normed_ref[...]), first_kept_ref[...])
    down, across = positions(order)
    rows_of = order.first_rows(lax.axis_index("seq"), order.received(across), across)
    first = exact(one_hot(rows_of == down, jnp.float32), first)
    for k, rows in enumerate(chunks(order.row_count, order.local_blocks)):
        first_ref[k] = first[rows, rows]


def call(kernel, name, outs, operands):
    return pl.pallas_call(
        kernel,
        in_specs=[WHOLE] * len(operands),
        out_specs=[WHOLE] * len(outs),
        out_shape=outs,
        compiler_params=granted(4),
        name=name,
    )(*operands)


def per_device(section_inputs, cotangent, gain, w_gate, w_out, mix_first, mix_second):
    inputs = section_inputs[0]
    local_blocks, block_rows = mix_first.shape[1:3]
    section_count = lax.axis_size("pipe")
    order = Order(inputs.shape[0], local_blocks, block_rows, lax.axis_size("seq"))

    (
        normed, inv_rms, first_recv, second_send, second_recv,
        mix_factor, slope, delta_hidden, kept, give,
    ) = begin(
        order, inputs, gain, mix_first[0], mix_second[0], w_gate[0], cotangent, w_out[0]
    )
    arrived = order.exchange(kept, give, streams=2)
    gate_turned, *out_turned = transposed(w_gate[0], w_out[0], arrived[0])
    moved, delta_mid, gate_factor, *outgoing = finish(
        order, *arrived, second_recv, first_recv, slope, delta_hidden, gate_turned, gain,
        inputs, inv_rms, cotangent,
    )

    row_count, width = inputs.shape
    short = array_of((row_count, width), jnp.bfloat16)
    square = array_of((row_count, row_count), jnp.float32)
    blocks = array_of((local_blocks, block_rows, block_rows), jnp.float32)
    kept = (delta_hidden, mix_factor)
    for sender in reversed(range(section_count - 1)):
        before = (delta_mid, *outgoing)
        incoming = [passed_down(part, sender + 1) for part in outgoing]
        delta_hidden = sum(dot(part, weight) for part, weight in zip(incoming, out_turned))
        delta_mix = (delta_hidden * mix_factor).astype(jnp.bfloat16)
        send = rounded(second_send, delta_mix)
        arrived = order.exchange(*jnp.split(send, 2))
        before_mid, *before_outgoing = before
        if sender + 2 == section_count:
            kept = call(
                functools.partial(keep_first_kernel, order, sender), "keep", [short, square, square],
                (arrived[0], normed, moved, before_mid, delta_mix, *kept, *before_outgoing),
            )
        else:
            kept = call(
                functools.partial(keep_kernel, order, sender), "keep",
                [short, square, square if sender else blocks],
                (arrived[0], normed, moved, before_mid, delta_mix, *before_outgoing, *kept),
            )
        delta_mid = jnp.concatenate(arrived)
        delta_gate = (delta_hidden * gate_factor).astype(jnp.bfloat16)
        gate_back = dot(delta_gate, gate_turned)
        if sender > 0:
            outgoing = advance(incoming, kept[1], delta_mid, first_recv, gate_back, gain, inputs, inv_rms)
    outgoing_kept, first_kept, grad_second = kept
    grad_inputs, grad_first = call(
        functools.partial(close_kernel, order), "close", [short, blocks],
        (
            delta_mid, first_recv, gate_back, gain, inputs, inv_rms, normed, *incoming,
            outgoing_kept, first_kept,
        ),
    )
    return (grad_inputs[None], grad_first[None], grad_second[None])


def solution(mesh):
    placed = (
        P("pipe", "seq", None),
        P("seq", None),
        P("pipe", None),
        P("pipe", None, None),
        P("pipe", None, None),
        P("pipe", "seq", None, None),
        P("pipe", "seq", None, None),
    )
    return jax.shard_map(
        per_device,
        mesh=mesh,
        in_specs=placed,
        out_specs=(
            P("pipe", "seq", None),
            P("pipe", "seq", None, None),
            P("pipe", "seq", None, None),
        ),
        check_vma=False,
    )
```

```python
import functools

import jax
import jax.numpy as jnp
from jax import lax
from jax.experimental import pallas as pl
from jax.experimental.pallas import tpu as pltpu
from jax.sharding import PartitionSpec as P

ROWS_BY_ROWS = (((1,), (1,)), ((), ()))
WHOLE = pl.BlockSpec(memory_space=pltpu.VMEM)
ANYWHERE = pl.BlockSpec(memory_space=pl.ANY)
HALVES = 2


def granted(mebibytes):
    return pltpu.CompilerParams(vmem_limit_bytes=mebibytes << 20)


def in_hbm(array):
    return pltpu.with_memory_space_constraint(array, pltpu.HBM)


def array_of(shape, dtype):
    return jax.ShapeDtypeStruct(shape, dtype)


def dot(left, right):
    return jnp.dot(left, right, preferred_element_type=jnp.float32)


def dot_rows(left, right):
    return lax.dot_general(left, right, ROWS_BY_ROWS, preferred_element_type=jnp.float32)


def swap(block, offset):
    count = lax.axis_size("seq")
    return lax.ppermute(block, "seq", [(i, i ^ offset) for i in range(count)])


def passed_down(block, sender):
    sections = lax.axis_size("pipe")
    pairs = []
    for device in range(lax.axis_size("seq")):
        for section in range(sections):
            target = (device ^ 1, section)
            if section in (sender, sender - 1):
                target = (device, 2 * sender - 1 - section)
            pairs.append((device * sections + section, target[0] * sections + target[1]))
    return lax.ppermute(block, ("seq", "pipe"), pairs)


def chunks(size, count):
    return [slice(i * size // count, (i + 1) * size // count) for i in range(count)]


def column_parts(width):
    cut = width // 3 // 128 * 128
    return [slice(0, cut), slice(cut, width)]


def log2(size):
    assert size & (size - 1) == 0
    return size.bit_length() - 1


class Order:
    def __init__(self, row_count, local_blocks, block_rows, seq_count):
        self.row_count = row_count
        self.local_blocks = local_blocks
        self.block_rows = block_rows
        self.seq_count = seq_count
        self.chips = seq_count // 2
        self.steps = block_rows // seq_count
        self.piece = local_blocks * self.steps

    def rows(self, group, count=1):
        return slice(group * self.piece, (group + count) * self.piece)

    def sent(self, position):
        group = position >> log2(self.piece)
        return (group >> log2(self.chips)) + 2 * (group & (self.chips - 1))

    def received(self, position):
        return position >> log2(self.piece)

    def first_rows(self, me, partner, position):
        block = (position >> log2(self.steps)) & (self.local_blocks - 1)
        step = position & (self.steps - 1)
        return block * self.block_rows + (me ^ partner) * self.steps + step

    def second_rows(self, me, partner, position):
        block = (position >> log2(self.steps)) & (self.local_blocks - 1)
        step = position & (self.steps - 1)
        return (step * self.seq_count + (me ^ partner)) * self.local_blocks + block

    def exchange(self, kept, give, streams=1):
        got = swap(give, 1)
        arrived = []
        for chip in range(self.chips):
            rows = self.rows(chip * streams, streams)
            message = jnp.concatenate([kept[rows], got[rows]])
            arrived.append(swap(message, 2 * chip) if chip else message)
        return arrived


def block_diagonal(blocks):
    zero = jnp.zeros(blocks[0].shape, blocks[0].dtype)
    return jnp.concatenate(
        [
            jnp.concatenate([b if k == j else zero for j in range(len(blocks))], axis=1)
            for k, b in enumerate(blocks)
        ],
        axis=0,
    )


def positions(order):
    square = (order.row_count, order.row_count)
    return lax.broadcasted_iota(jnp.int32, square, 0), lax.broadcasted_iota(jnp.int32, square, 1)


def one_hot(matches, dtype=jnp.bfloat16):
    return jnp.where(matches, 1.0, 0.0).astype(dtype)


def rounded(left, right):
    return dot(left, right).astype(jnp.bfloat16)


def begin_kernel(
    order, x_hbm, gain_hbm, first_hbm, second_hbm, gate_hbm, incoming_hbm, out_hbm,
    normed_ref, inv_ref, first_recv_ref, second_send_ref, second_recv_ref,
    mix_factor_ref, slope_ref, hidden_ref, keep_ref, give_ref,
    x_ref, gain_ref, first_ref, second_ref, gate_ref, incoming_ref, out_ref, sems,
):
    parts = chunks(out_hbm.shape[0], sems.shape[0] - 6)
    pairs = [(first_hbm, first_ref), (second_hbm, second_ref), (x_hbm, x_ref), (gain_hbm, gain_ref)]
    pairs += [(gate_hbm, gate_ref), (incoming_hbm, incoming_ref)]
    pairs += [(out_hbm.at[rows], out_ref.at[rows]) for rows in parts]
    copies = [pltpu.make_async_copy(*pair, sems.at[i]) for i, pair in enumerate(pairs)]
    for copy in copies[:5]:
        copy.start()
    active = lax.axis_index("pipe") == lax.axis_size("pipe") - 1

    @pl.when(active)
    def _():
        for copy in copies[5:]:
            copy.start()

    me = lax.axis_index("seq")
    down, across = positions(order)
    sent, received = order.sent(down), order.received(across)
    first_sent = one_hot(order.first_rows(me, sent, down) == across)
    second_sent = one_hot(order.second_rows(me, sent, down) == across)
    first_received = one_hot(order.first_rows(me, received, across) == down)
    second_received = one_hot(order.second_rows(me, received, across) == down)
    for copy in copies[:2]:
        copy.wait()
    first = block_diagonal([first_ref[k].astype(jnp.float32) for k in range(order.local_blocks)])
    second = block_diagonal([second_ref[k].astype(jnp.float32) for k in range(order.local_blocks)])
    first_send = rounded(first_sent, first.astype(jnp.bfloat16))
    second_send_ref[...] = rounded(second_sent, second.T.astype(jnp.bfloat16))
    first_recv_ref[...] = rounded(first.T.astype(jnp.bfloat16), first_received)
    second_recv_ref[...] = rounded(second.astype(jnp.bfloat16), second_received)
    for copy in copies[2:4]:
        copy.wait()
    features = x_ref[...].astype(jnp.float32)
    inv_rms = lax.rsqrt(jnp.mean(features * features, axis=-1, keepdims=True) + 1e-06)
    inv_ref[...] = inv_rms
    normed = (features * inv_rms * gain_ref[...]).astype(jnp.bfloat16)
    normed_ref[...] = normed

    def place(send, stream, columns):
        for core, target in enumerate((keep_ref, give_ref)):
            for chip in range(order.chips):
                rows = order.rows(2 * chip + stream)
                target[rows, columns] = send[order.rows(core * order.chips + chip)]

    place(rounded(first_send, normed), 0, slice(None))
    copies[4].wait()
    gate_pre = dot(normed, gate_ref[...])
    sigma = jax.nn.sigmoid(gate_pre)
    mix_factor_ref[...] = gate_pre * sigma
    slope_ref[...] = sigma * (1.0 + gate_pre * (1.0 - sigma))

    @pl.when(active)
    def _():
        copies[5].wait()
        for columns, copy in zip(parts, copies[6:]):
            copy.wait()
            hidden_ref[:, columns] = dot_rows(incoming_ref[...], out_ref[columns])
        mix = (hidden_ref[...] * mix_factor_ref[...]).astype(jnp.bfloat16)
        place(rounded(second_send_ref[...], mix), 1, slice(None))

    @pl.when(jnp.logical_not(active))
    def _():
        hidden_ref[...] = jnp.zeros(hidden_ref.shape, hidden_ref.dtype)
        place(jnp.zeros(normed_ref.shape, normed_ref.dtype), 1, slice(None))


def begin(order, *operands):
    row_count, width = operands[0].shape
    square = array_of((row_count, row_count), jnp.bfloat16)
    short = array_of((row_count, width), jnp.bfloat16)
    full = array_of((row_count, width), jnp.float32)
    column = array_of((row_count, 1), jnp.float32)
    outs = [short, column, square, square, square, full, full, full, short, short]
    return pl.pallas_call(
        functools.partial(begin_kernel, order),
        in_specs=[ANYWHERE] * len(operands),
        out_specs=[WHOLE] * len(outs),
        out_shape=outs,
        scratch_shapes=[pltpu.VMEM(o.shape, o.dtype) for o in operands]
        + [pltpu.SemaphoreType.DMA((9,))],
        compiler_params=granted(13),
        name="begin",
    )(*[in_hbm(o) for o in operands])


def transpose_kernel(gate_hbm, out_hbm, after_ref, gate_turned_ref, *refs):
    out_turned_refs, (gate_held, out_held, sems) = refs[:-3], refs[-3:]
    parts = chunks(gate_held.shape[0], sems.shape[1])
    work = []
    for i, (source, held) in enumerate(((gate_hbm, gate_held), (out_hbm, out_held))):
        for j, rows in enumerate(parts):
            copy = pltpu.make_async_copy(source.at[rows], held.at[rows], sems.at[i, j])
            copy.start()
            work.append((copy, held, rows, [gate_turned_ref] if i == 0 else out_turned_refs))
    for copy, held, rows, targets in work:
        copy.wait()
        width = held.shape[1]
        columns_of = column_parts(width) if len(targets) > 1 else [slice(0, width)]
        for target, columns in zip(targets, columns_of):
            target[:, rows] = held[rows, columns].T


def transposed(weight_gate, weight_out, after):
    height, width = weight_out.shape
    parts = [pltpu.VMEM((c.stop - c.start, height), jnp.bfloat16) for c in column_parts(width)]
    return pl.pallas_call(
        transpose_kernel,
        in_specs=[ANYWHERE] * 3,
        out_specs=[WHOLE] * (1 + HALVES),
        out_shape=[pltpu.VMEM(weight_gate.shape[::-1], jnp.bfloat16)] + parts,
        scratch_shapes=[
            pltpu.VMEM(weight_gate.shape, weight_gate.dtype),
            pltpu.VMEM(weight_out.shape, weight_out.dtype),
            pltpu.SemaphoreType.DMA((2, 6)),
        ],
        compiler_params=granted(11),
        name="transposed",
    )(in_hbm(weight_gate), in_hbm(weight_out), after)


def joined(refs):
    return jnp.concatenate([ref[...] for ref in refs], axis=1)


def store_halves(refs, value):
    for ref, columns in zip(refs, column_parts(value.shape[1])):
        ref[...] = value[:, columns]


def outgoing_of(gate_back, first_back, gain, inputs, inv_rms, incoming):
    delta_norm = (first_back + gate_back) * gain
    unit_rows = inputs.astype(jnp.float32) * inv_rms
    centred = delta_norm - unit_rows * jnp.mean(delta_norm * unit_rows, axis=-1, keepdims=True)
    return (incoming.astype(jnp.float32) + inv_rms * centred).astype(jnp.bfloat16)


def finish_kernel(order, *refs):
    arrived, refs = refs[: order.chips], refs[order.chips :]
    (
        second_recv_ref, first_recv_ref, slope_ref, hidden_ref, gate_ref, gain_ref, x_ref, inv_ref,
        incoming_ref, moved_ref, mid_ref, gate_factor_ref, *outgoing_refs,
    ) = refs
    for chip, message in enumerate(arrived):
        for core in range(2):
            for stream, target in enumerate((moved_ref, mid_ref)):
                target[order.rows(2 * chip + core)] = message[order.rows(2 * core + stream)]
    gate_factor = dot(second_recv_ref[...], moved_ref[...]) * slope_ref[...]
    gate_factor_ref[...] = gate_factor
    delta_gate = (hidden_ref[...] * gate_factor).astype(jnp.bfloat16)
    gate_back = dot(delta_gate, gate_ref[...])
    first_back = dot(first_recv_ref[...], mid_ref[...])
    outgoing = outgoing_of(
        gate_back, first_back, gain_ref[...], x_ref[...], inv_ref[...], incoming_ref[...]
    )
    store_halves(outgoing_refs, outgoing)


def finish(order, *operands):
    row_count, width = operands[-1].shape
    short = array_of((row_count, width), jnp.bfloat16)
    full = array_of((row_count, width), jnp.float32)
    parts = [array_of((row_count, c.stop - c.start), jnp.bfloat16) for c in column_parts(width)]
    return pl.pallas_call(
        functools.partial(finish_kernel, order),
        in_specs=[WHOLE] * len(operands),
        out_specs=[WHOLE] * (3 + HALVES),
        out_shape=[short, short, full] + parts,
        compiler_params=granted(4),
        name="finish",
    )(*operands)


def mix_kernel(
    partial_ref, last_ref, weight_ref, mix_factor_ref, gate_factor_ref, second_send_ref,
    mix_ref, gate_ref, keep_ref, give_ref,
):
    hidden = partial_ref[...] + dot(last_ref[...], weight_ref[...])
    mix = (hidden * mix_factor_ref[...]).astype(jnp.bfloat16)
    mix_ref[...] = mix
    send = rounded(second_send_ref[...], mix)
    half = keep_ref.shape[0]
    keep_ref[...] = send[:half]
    give_ref[...] = send[half:]
    gate_ref[...] = (hidden * gate_factor_ref[...]).astype(jnp.bfloat16)


def advance_kernel(
    after_ref, mid_ref, first_recv_ref, gate_back_ref, gain_ref, x_ref, inv_ref, *refs
):
    incoming_refs, outgoing_refs = refs[:HALVES], refs[HALVES:]
    first_back = dot(first_recv_ref[...], mid_ref[...])
    outgoing = outgoing_of(
        gate_back_ref[...], first_back, gain_ref[...], x_ref[...], inv_ref[...],
        joined(incoming_refs),
    )
    store_halves(outgoing_refs, outgoing)


def advance(incoming, *operands):
    return pl.pallas_call(
        advance_kernel,
        in_specs=[WHOLE] * (len(operands) + HALVES),
        out_specs=[WHOLE] * HALVES,
        out_shape=[array_of(part.shape, part.dtype) for part in incoming],
        compiler_params=granted(4),
        name="advance",
    )(*operands, *incoming)


def exact(left, right):
    return jnp.dot(
        left, right, precision=lax.Precision.HIGHEST, preferred_element_type=jnp.float32
    )


def keep_kernel(order, section, after_ref, normed_ref, moved_ref, mid_ref, mix_ref, *refs):
    outgoing_refs, kept, new = refs[:HALVES], refs[HALVES : HALVES + 3], refs[HALVES + 3 :]
    index = lax.axis_index("pipe")
    new[0][...] = jnp.where(index == section + 1, joined(outgoing_refs), kept[0][...])
    first = dot_rows(mid_ref[...], normed_ref[...])
    new[1][...] = jnp.where(index == section + 1, first, kept[1][...])
    second = dot_rows(mix_ref[...], moved_ref[...])
    second = jnp.where(index == section, second, kept[2][...])
    if section > 0:
        new[2][...] = second
        return
    down, across = positions(order)
    rows_of = order.second_rows(lax.axis_index("seq"), order.received(down), down)
    second = exact(second, one_hot(rows_of == across, jnp.float32))
    for k, rows in enumerate(chunks(order.row_count, order.local_blocks)):
        new[2][k] = second[rows, rows]


def keep_first_kernel(
    order, section, after_ref, normed_ref, moved_ref, mid_ref, mix_ref, hidden_ref, mix_factor_ref, *refs
):
    outgoing_refs, new = refs[:HALVES], refs[HALVES:]
    new[0][...] = joined(outgoing_refs)
    new[1][...] = dot_rows(mid_ref[...], normed_ref[...])
    before = (hidden_ref[...] * mix_factor_ref[...]).astype(jnp.bfloat16)
    mix = jnp.where(lax.axis_index("pipe") == section, mix_ref[...], before)
    new[2][...] = dot_rows(mix, moved_ref[...])


def close_kernel(
    order, mid_ref, first_recv_ref, gate_back_ref, gain_ref, x_ref, inv_ref, normed_ref, *refs
):
    incoming_refs, refs = refs[:HALVES], refs[HALVES:]
    outgoing_kept_ref, first_kept_ref, outgoing_ref, first_ref = refs
    active = lax.axis_index("pipe") == 0
    first_back = dot(first_recv_ref[...], mid_ref[...])
    outgoing = outgoing_of(
        gate_back_ref[...], first_back, gain_ref[...], x_ref[...], inv_ref[...],
        joined(incoming_refs),
    )
    outgoing_ref[...] = jnp.where(active, outgoing, outgoing_kept_ref[...])
    first = jnp.where(active, dot_rows(mid_ref[...], normed_ref[...]), first_kept_ref[...])
    down, across = positions(order)
    rows_of = order.first_rows(lax.axis_index("seq"), order.received(across), across)
    first = exact(one_hot(rows_of == down, jnp.float32), first)
    for k, rows in enumerate(chunks(order.row_count, order.local_blocks)):
        first_ref[k] = first[rows, rows]


def call(kernel, name, outs, operands):
    return pl.pallas_call(
        kernel,
        in_specs=[WHOLE] * len(operands),
        out_specs=[WHOLE] * len(outs),
        out_shape=outs,
        compiler_params=granted(4),
        name=name,
    )(*operands)


def per_device(section_inputs, cotangent, gain, w_gate, w_out, mix_first, mix_second):
    inputs = section_inputs[0]
    local_blocks, block_rows = mix_first.shape[1:3]
    section_count = lax.axis_size("pipe")
    order = Order(inputs.shape[0], local_blocks, block_rows, lax.axis_size("seq"))

    (
        normed, inv_rms, first_recv, second_send, second_recv,
        mix_factor, slope, delta_hidden, kept, give,
    ) = begin(
        order, inputs, gain, mix_first[0], mix_second[0], w_gate[0], cotangent, w_out[0]
    )
    arrived = order.exchange(kept, give, streams=2)
    gate_turned, *out_turned = transposed(w_gate[0], w_out[0], arrived[0])
    moved, delta_mid, gate_factor, *outgoing = finish(
        order, *arrived, second_recv, first_recv, slope, delta_hidden, gate_turned, gain,
        inputs, inv_rms, cotangent,
    )

    row_count, width = inputs.shape
    short = array_of((row_count, width), jnp.bfloat16)
    half = array_of((row_count // 2, width), jnp.bfloat16)
    square = array_of((row_count, row_count), jnp.float32)
    blocks = array_of((local_blocks, block_rows, block_rows), jnp.float32)
    kept = (delta_hidden, mix_factor)
    for sender in reversed(range(section_count - 1)):
        before = (delta_mid, *outgoing)
        incoming = [passed_down(part, sender + 1) for part in outgoing]
        last, *first = zip(incoming, out_turned)
        partial = sum(dot(part, weight) for part, weight in first)
        delta_mix, delta_gate, kept_pieces, give = call(
            mix_kernel, "mix", [short, short, half, half],
            (partial, *last, mix_factor, gate_factor, second_send),
        )
        arrived = order.exchange(kept_pieces, give)
        before_mid, *before_outgoing = before
        if sender + 2 == section_count:
            kept = call(
                functools.partial(keep_first_kernel, order, sender), "keep", [short, square, square],
                (arrived[0], normed, moved, before_mid, delta_mix, *kept, *before_outgoing),
            )
        else:
            kept = call(
                functools.partial(keep_kernel, order, sender), "keep",
                [short, square, square if sender else blocks],
                (arrived[0], normed, moved, before_mid, delta_mix, *before_outgoing, *kept),
            )
        delta_mid = jnp.concatenate(arrived)
        gate_back = dot(delta_gate, gate_turned)
        if sender > 0:
            outgoing = advance(incoming, kept[1], delta_mid, first_recv, gate_back, gain, inputs, inv_rms)
    outgoing_kept, first_kept, grad_second = kept
    grad_inputs, grad_first = call(
        functools.partial(close_kernel, order), "close", [short, blocks],
        (
            delta_mid, first_recv, gate_back, gain, inputs, inv_rms, normed, *incoming,
            outgoing_kept, first_kept,
        ),
    )
    return (grad_inputs[None], grad_first[None], grad_second[None])


def solution(mesh):
    placed = (
        P("pipe", "seq", None),
        P("seq", None),
        P("pipe", None),
        P("pipe", None, None),
        P("pipe", None, None),
        P("pipe", "seq", None, None),
        P("pipe", "seq", None, None),
    )
    return jax.shard_map(
        per_device,
        mesh=mesh,
        in_specs=placed,
        out_specs=(
            P("pipe", "seq", None),
            P("pipe", "seq", None, None),
            P("pipe", "seq", None, None),
        ),
        check_vma=False,
    )
```

```python
import functools

import jax
import jax.numpy as jnp
from jax import lax
from jax.experimental import pallas as pl
from jax.experimental.pallas import tpu as pltpu
from jax.sharding import PartitionSpec as P

ROWS_BY_ROWS = (((1,), (1,)), ((), ()))
WHOLE = pl.BlockSpec(memory_space=pltpu.VMEM)
ANYWHERE = pl.BlockSpec(memory_space=pl.ANY)
HALVES = 2


def granted(mebibytes):
    return pltpu.CompilerParams(vmem_limit_bytes=mebibytes << 20)


def in_hbm(array):
    return pltpu.with_memory_space_constraint(array, pltpu.HBM)


def array_of(shape, dtype):
    return jax.ShapeDtypeStruct(shape, dtype)


def dot(left, right):
    return jnp.dot(left, right, preferred_element_type=jnp.float32)


def dot_rows(left, right):
    return lax.dot_general(left, right, ROWS_BY_ROWS, preferred_element_type=jnp.float32)


def swap(block, offset):
    count = lax.axis_size("seq")
    return lax.ppermute(block, "seq", [(i, i ^ offset) for i in range(count)])


def passed_down(block, sender):
    sections = lax.axis_size("pipe")
    pairs = []
    for device in range(lax.axis_size("seq")):
        for section in range(sections):
            target = (device ^ 1, section)
            if section in (sender, sender - 1):
                target = (device, 2 * sender - 1 - section)
            pairs.append((device * sections + section, target[0] * sections + target[1]))
    return lax.ppermute(block, ("seq", "pipe"), pairs)


def chunks(size, count):
    return [slice(i * size // count, (i + 1) * size // count) for i in range(count)]


def column_parts(width):
    cut = width // 3 // 128 * 128
    return [slice(0, cut), slice(cut, width)]


def log2(size):
    assert size & (size - 1) == 0
    return size.bit_length() - 1


class Order:
    def __init__(self, row_count, local_blocks, block_rows, seq_count):
        self.row_count = row_count
        self.local_blocks = local_blocks
        self.block_rows = block_rows
        self.seq_count = seq_count
        self.chips = seq_count // 2
        self.steps = block_rows // seq_count
        self.piece = local_blocks * self.steps

    def rows(self, group, count=1):
        return slice(group * self.piece, (group + count) * self.piece)

    def sent(self, position):
        group = position >> log2(self.piece)
        return (group >> log2(self.chips)) + 2 * (group & (self.chips - 1))

    def received(self, position):
        return position >> log2(self.piece)

    def first_rows(self, me, partner, position):
        block = (position >> log2(self.steps)) & (self.local_blocks - 1)
        step = position & (self.steps - 1)
        return block * self.block_rows + (me ^ partner) * self.steps + step

    def second_rows(self, me, partner, position):
        block = (position >> log2(self.steps)) & (self.local_blocks - 1)
        step = position & (self.steps - 1)
        return (step * self.seq_count + (me ^ partner)) * self.local_blocks + block

    def given(self, chip):
        return (0, 0) if chip == 1 else (1, max(chip - 1, 0))

    def exchange(self, kept, give, streams=1):
        got = [swap(part, 1) for part in give]
        arrived = []
        for chip in range(self.chips):
            part, index = self.given(chip)
            own = kept[self.rows(chip * streams, streams)]
            message = jnp.concatenate([own, got[part][self.rows(index * streams, streams)]])
            arrived.append(swap(message, 2 * chip) if chip else message)
        return arrived


def block_diagonal(blocks):
    zero = jnp.zeros(blocks[0].shape, blocks[0].dtype)
    return jnp.concatenate(
        [
            jnp.concatenate([b if k == j else zero for j in range(len(blocks))], axis=1)
            for k, b in enumerate(blocks)
        ],
        axis=0,
    )


def positions(order):
    square = (order.row_count, order.row_count)
    return lax.broadcasted_iota(jnp.int32, square, 0), lax.broadcasted_iota(jnp.int32, square, 1)


def one_hot(matches, dtype=jnp.bfloat16):
    return jnp.where(matches, 1.0, 0.0).astype(dtype)


def rounded(left, right):
    return dot(left, right).astype(jnp.bfloat16)


def begin_kernel(
    order, x_hbm, gain_hbm, first_hbm, second_hbm, gate_hbm, incoming_hbm, out_hbm,
    normed_ref, inv_ref, first_recv_ref, second_send_ref, second_recv_ref,
    mix_factor_ref, slope_ref, hidden_ref, keep_ref, give_first_ref, give_rest_ref,
    x_ref, gain_ref, first_ref, second_ref, gate_ref, incoming_ref, out_ref, sems,
):
    parts = chunks(out_hbm.shape[0], sems.shape[0] - 6)
    pairs = [(first_hbm, first_ref), (second_hbm, second_ref), (x_hbm, x_ref), (gain_hbm, gain_ref)]
    pairs += [(gate_hbm, gate_ref), (incoming_hbm, incoming_ref)]
    pairs += [(out_hbm.at[rows], out_ref.at[rows]) for rows in parts]
    copies = [pltpu.make_async_copy(*pair, sems.at[i]) for i, pair in enumerate(pairs)]
    for copy in copies[:5]:
        copy.start()
    active = lax.axis_index("pipe") == lax.axis_size("pipe") - 1

    @pl.when(active)
    def _():
        for copy in copies[5:]:
            copy.start()

    me = lax.axis_index("seq")
    down, across = positions(order)
    sent, received = order.sent(down), order.received(across)
    first_sent = one_hot(order.first_rows(me, sent, down) == across)
    second_sent = one_hot(order.second_rows(me, sent, down) == across)
    first_received = one_hot(order.first_rows(me, received, across) == down)
    second_received = one_hot(order.second_rows(me, received, across) == down)
    for copy in copies[:2]:
        copy.wait()
    first = block_diagonal([first_ref[k].astype(jnp.float32) for k in range(order.local_blocks)])
    second = block_diagonal([second_ref[k].astype(jnp.float32) for k in range(order.local_blocks)])
    first_send = rounded(first_sent, first.astype(jnp.bfloat16))
    second_send_ref[...] = rounded(second_sent, second.T.astype(jnp.bfloat16))
    first_recv_ref[...] = rounded(first.T.astype(jnp.bfloat16), first_received)
    second_recv_ref[...] = rounded(second.astype(jnp.bfloat16), second_received)
    for copy in copies[2:4]:
        copy.wait()
    features = x_ref[...].astype(jnp.float32)
    inv_rms = lax.rsqrt(jnp.mean(features * features, axis=-1, keepdims=True) + 1e-06)
    inv_ref[...] = inv_rms
    normed = (features * inv_rms * gain_ref[...]).astype(jnp.bfloat16)
    normed_ref[...] = normed

    def place(send, stream, columns):
        for chip in range(order.chips):
            keep_ref[order.rows(2 * chip + stream), columns] = send[order.rows(chip)]
            part, index = order.given(chip)
            target = (give_first_ref, give_rest_ref)[part]
            target[order.rows(2 * index + stream), columns] = send[order.rows(order.chips + chip)]

    place(rounded(first_send, normed), 0, slice(None))
    copies[4].wait()
    gate_pre = dot(normed, gate_ref[...])
    sigma = jax.nn.sigmoid(gate_pre)
    mix_factor_ref[...] = gate_pre * sigma
    slope_ref[...] = sigma * (1.0 + gate_pre * (1.0 - sigma))

    @pl.when(active)
    def _():
        copies[5].wait()
        for columns, copy in zip(parts, copies[6:]):
            copy.wait()
            hidden_ref[:, columns] = dot_rows(incoming_ref[...], out_ref[columns])
        mix = (hidden_ref[...] * mix_factor_ref[...]).astype(jnp.bfloat16)
        place(rounded(second_send_ref[...], mix), 1, slice(None))

    @pl.when(jnp.logical_not(active))
    def _():
        hidden_ref[...] = jnp.zeros(hidden_ref.shape, hidden_ref.dtype)
        place(jnp.zeros(normed_ref.shape, normed_ref.dtype), 1, slice(None))


def begin(order, *operands):
    row_count, width = operands[0].shape
    square = array_of((row_count, row_count), jnp.bfloat16)
    short = array_of((row_count, width), jnp.bfloat16)
    full = array_of((row_count, width), jnp.float32)
    column = array_of((row_count, 1), jnp.float32)
    give = [array_of((2 * order.piece * n, width), jnp.bfloat16) for n in (1, order.chips - 1)]
    outs = [short, column, square, square, square, full, full, full, short, *give]
    return pl.pallas_call(
        functools.partial(begin_kernel, order),
        in_specs=[ANYWHERE] * len(operands),
        out_specs=[WHOLE] * len(outs),
        out_shape=outs,
        scratch_shapes=[pltpu.VMEM(o.shape, o.dtype) for o in operands]
        + [pltpu.SemaphoreType.DMA((9,))],
        compiler_params=granted(13),
        name="begin",
    )(*[in_hbm(o) for o in operands])


def transpose_kernel(gate_hbm, out_hbm, after_ref, gate_turned_ref, *refs):
    out_turned_refs, (gate_held, out_held, sems) = refs[:-3], refs[-3:]
    parts = chunks(gate_held.shape[0], sems.shape[1])
    work = []
    for i, (source, held) in enumerate(((gate_hbm, gate_held), (out_hbm, out_held))):
        for j, rows in enumerate(parts):
            copy = pltpu.make_async_copy(source.at[rows], held.at[rows], sems.at[i, j])
            copy.start()
            work.append((copy, held, rows, [gate_turned_ref] if i == 0 else out_turned_refs))
    for copy, held, rows, targets in work:
        copy.wait()
        width = held.shape[1]
        columns_of = column_parts(width) if len(targets) > 1 else [slice(0, width)]
        for target, columns in zip(targets, columns_of):
            target[:, rows] = held[rows, columns].T


def transposed(weight_gate, weight_out, after):
    height, width = weight_out.shape
    parts = [pltpu.VMEM((c.stop - c.start, height), jnp.bfloat16) for c in column_parts(width)]
    return pl.pallas_call(
        transpose_kernel,
        in_specs=[ANYWHERE] * 3,
        out_specs=[WHOLE] * (1 + HALVES),
        out_shape=[pltpu.VMEM(weight_gate.shape[::-1], jnp.bfloat16)] + parts,
        scratch_shapes=[
            pltpu.VMEM(weight_gate.shape, weight_gate.dtype),
            pltpu.VMEM(weight_out.shape, weight_out.dtype),
            pltpu.SemaphoreType.DMA((2, 6)),
        ],
        compiler_params=granted(11),
        name="transposed",
    )(in_hbm(weight_gate), in_hbm(weight_out), after)


def joined(refs):
    return jnp.concatenate([ref[...] for ref in refs], axis=1)


def store_halves(refs, value):
    for ref, columns in zip(refs, column_parts(value.shape[1])):
        ref[...] = value[:, columns]


def outgoing_of(gate_back, first_back, gain, inputs, inv_rms, incoming):
    delta_norm = (first_back + gate_back) * gain
    unit_rows = inputs.astype(jnp.float32) * inv_rms
    centred = delta_norm - unit_rows * jnp.mean(delta_norm * unit_rows, axis=-1, keepdims=True)
    return (incoming.astype(jnp.float32) + inv_rms * centred).astype(jnp.bfloat16)


def finish_kernel(order, *refs):
    arrived, refs = refs[: order.chips], refs[order.chips :]
    (
        second_recv_ref, first_recv_ref, slope_ref, hidden_ref, gate_ref, gain_ref, x_ref, inv_ref,
        incoming_ref, moved_ref, mid_ref, gate_factor_ref, *outgoing_refs,
    ) = refs
    for chip, message in enumerate(arrived):
        for core in range(2):
            for stream, target in enumerate((moved_ref, mid_ref)):
                target[order.rows(2 * chip + core)] = message[order.rows(2 * core + stream)]
    gate_factor = dot(second_recv_ref[...], moved_ref[...]) * slope_ref[...]
    gate_factor_ref[...] = gate_factor
    delta_gate = (hidden_ref[...] * gate_factor).astype(jnp.bfloat16)
    gate_back = dot(delta_gate, gate_ref[...])
    first_back = dot(first_recv_ref[...], mid_ref[...])
    outgoing = outgoing_of(
        gate_back, first_back, gain_ref[...], x_ref[...], inv_ref[...], incoming_ref[...]
    )
    store_halves(outgoing_refs, outgoing)


def finish(order, *operands):
    row_count, width = operands[-1].shape
    short = array_of((row_count, width), jnp.bfloat16)
    full = array_of((row_count, width), jnp.float32)
    parts = [array_of((row_count, c.stop - c.start), jnp.bfloat16) for c in column_parts(width)]
    return pl.pallas_call(
        functools.partial(finish_kernel, order),
        in_specs=[WHOLE] * len(operands),
        out_specs=[WHOLE] * (3 + HALVES),
        out_shape=[short, short, full] + parts,
        compiler_params=granted(4),
        name="finish",
    )(*operands)


def mix_kernel(
    order, partial_ref, last_ref, weight_ref, mix_factor_ref, gate_factor_ref, second_send_ref,
    mix_ref, gate_ref, keep_ref, *give_refs,
):
    hidden = partial_ref[...] + dot(last_ref[...], weight_ref[...])
    mix = (hidden * mix_factor_ref[...]).astype(jnp.bfloat16)
    mix_ref[...] = mix
    send = rounded(second_send_ref[...], mix)
    keep_ref[...] = send[: keep_ref.shape[0]]
    for chip in range(order.chips):
        part, index = order.given(chip)
        give_refs[part][order.rows(index)] = send[order.rows(order.chips + chip)]
    gate_ref[...] = (hidden * gate_factor_ref[...]).astype(jnp.bfloat16)


def gate_kernel(after_ref, gate_ref, weight_ref, out_ref):
    out_ref[...] = dot(gate_ref[...], weight_ref[...])


def advance_kernel(
    after_ref, mid_ref, first_recv_ref, gate_back_ref, gain_ref, x_ref, inv_ref, *refs
):
    incoming_refs, outgoing_refs = refs[:HALVES], refs[HALVES:]
    first_back = dot(first_recv_ref[...], mid_ref[...])
    outgoing = outgoing_of(
        gate_back_ref[...], first_back, gain_ref[...], x_ref[...], inv_ref[...],
        joined(incoming_refs),
    )
    store_halves(outgoing_refs, outgoing)


def advance(incoming, *operands):
    return pl.pallas_call(
        advance_kernel,
        in_specs=[WHOLE] * (len(operands) + HALVES),
        out_specs=[WHOLE] * HALVES,
        out_shape=[array_of(part.shape, part.dtype) for part in incoming],
        compiler_params=granted(4),
        name="advance",
    )(*operands, *incoming)


def exact(left, right):
    return jnp.dot(
        left, right, precision=lax.Precision.HIGHEST, preferred_element_type=jnp.float32
    )


def keep_kernel(order, section, after_ref, normed_ref, moved_ref, mid_ref, mix_ref, *refs):
    outgoing_refs, kept, new = refs[:HALVES], refs[HALVES : HALVES + 3], refs[HALVES + 3 :]
    index = lax.axis_index("pipe")
    new[0][...] = jnp.where(index == section + 1, joined(outgoing_refs), kept[0][...])
    first = dot_rows(mid_ref[...], normed_ref[...])
    new[1][...] = jnp.where(index == section + 1, first, kept[1][...])
    second = dot_rows(mix_ref[...], moved_ref[...])
    second = jnp.where(index == section, second, kept[2][...])
    if section > 0:
        new[2][...] = second
        return
    down, across = positions(order)
    rows_of = order.second_rows(lax.axis_index("seq"), order.received(down), down)
    second = exact(second, one_hot(rows_of == across, jnp.float32))
    for k, rows in enumerate(chunks(order.row_count, order.local_blocks)):
        new[2][k] = second[rows, rows]


def keep_first_kernel(
    order, section, after_ref, normed_ref, moved_ref, mid_ref, mix_ref, hidden_ref, mix_factor_ref, *refs
):
    outgoing_refs, new = refs[:HALVES], refs[HALVES:]
    new[0][...] = joined(outgoing_refs)
    new[1][...] = dot_rows(mid_ref[...], normed_ref[...])
    before = (hidden_ref[...] * mix_factor_ref[...]).astype(jnp.bfloat16)
    mix = jnp.where(lax.axis_index("pipe") == section, mix_ref[...], before)
    new[2][...] = dot_rows(mix, moved_ref[...])


def close_kernel(
    order, mid_ref, first_recv_ref, gate_back_ref, gain_ref, x_ref, inv_ref, normed_ref, *refs
):
    incoming_refs, refs = refs[:HALVES], refs[HALVES:]
    outgoing_kept_ref, first_kept_ref, outgoing_ref, first_ref = refs
    active = lax.axis_index("pipe") == 0
    first_back = dot(first_recv_ref[...], mid_ref[...])
    outgoing = outgoing_of(
        gate_back_ref[...], first_back, gain_ref[...], x_ref[...], inv_ref[...],
        joined(incoming_refs),
    )
    outgoing_ref[...] = jnp.where(active, outgoing, outgoing_kept_ref[...])
    first = jnp.where(active, dot_rows(mid_ref[...], normed_ref[...]), first_kept_ref[...])
    down, across = positions(order)
    rows_of = order.first_rows(lax.axis_index("seq"), order.received(across), across)
    first = exact(one_hot(rows_of == down, jnp.float32), first)
    for k, rows in enumerate(chunks(order.row_count, order.local_blocks)):
        first_ref[k] = first[rows, rows]


def call(kernel, name, outs, operands):
    return pl.pallas_call(
        kernel,
        in_specs=[WHOLE] * len(operands),
        out_specs=[WHOLE] * len(outs),
        out_shape=outs,
        compiler_params=granted(4),
        name=name,
    )(*operands)


def per_device(section_inputs, cotangent, gain, w_gate, w_out, mix_first, mix_second):
    inputs = section_inputs[0]
    local_blocks, block_rows = mix_first.shape[1:3]
    section_count = lax.axis_size("pipe")
    order = Order(inputs.shape[0], local_blocks, block_rows, lax.axis_size("seq"))

    (
        normed, inv_rms, first_recv, second_send, second_recv,
        mix_factor, slope, delta_hidden, kept, *give,
    ) = begin(
        order, inputs, gain, mix_first[0], mix_second[0], w_gate[0], cotangent, w_out[0]
    )
    arrived = order.exchange(kept, give, streams=2)
    gate_turned, *out_turned = transposed(w_gate[0], w_out[0], arrived[0])
    moved, delta_mid, gate_factor, *outgoing = finish(
        order, *arrived, second_recv, first_recv, slope, delta_hidden, gate_turned, gain,
        inputs, inv_rms, cotangent,
    )

    row_count, width = inputs.shape
    short = array_of((row_count, width), jnp.bfloat16)
    full = array_of((row_count, width), jnp.float32)
    half = array_of((row_count // 2, width), jnp.bfloat16)
    pieces = [array_of((order.piece * n, width), jnp.bfloat16) for n in (1, order.chips - 1)]
    square = array_of((row_count, row_count), jnp.float32)
    blocks = array_of((local_blocks, block_rows, block_rows), jnp.float32)
    kept = (delta_hidden, mix_factor)
    for sender in reversed(range(section_count - 1)):
        before = (delta_mid, *outgoing)
        incoming = [passed_down(part, sender + 1) for part in outgoing]
        last, *first = zip(incoming, out_turned)
        partial = sum(dot(part, weight) for part, weight in first)
        delta_mix, delta_gate, kept_pieces, *give = call(
            functools.partial(mix_kernel, order), "mix", [short, short, half, *pieces],
            (partial, *last, mix_factor, gate_factor, second_send),
        )
        arrived = order.exchange(kept_pieces, give)
        before_mid, *before_outgoing = before
        if sender + 2 == section_count:
            kept = call(
                functools.partial(keep_first_kernel, order, sender), "keep", [short, square, square],
                (arrived[0], normed, moved, before_mid, delta_mix, *kept, *before_outgoing),
            )
        else:
            kept = call(
                functools.partial(keep_kernel, order, sender), "keep",
                [short, square, square if sender else blocks],
                (arrived[0], normed, moved, before_mid, delta_mix, *before_outgoing, *kept),
            )
        delta_mid = jnp.concatenate(arrived)
        (gate_back,) = call(gate_kernel, "gate", [full], (arrived[0], delta_gate, gate_turned))
        if sender > 0:
            outgoing = advance(incoming, kept[1], delta_mid, first_recv, gate_back, gain, inputs, inv_rms)
    outgoing_kept, first_kept, grad_second = kept
    grad_inputs, grad_first = call(
        functools.partial(close_kernel, order), "close", [short, blocks],
        (
            delta_mid, first_recv, gate_back, gain, inputs, inv_rms, normed, *incoming,
            outgoing_kept, first_kept,
        ),
    )
    return (grad_inputs[None], grad_first[None], grad_second[None])


def solution(mesh):
    placed = (
        P("pipe", "seq", None),
        P("seq", None),
        P("pipe", None),
        P("pipe", None, None),
        P("pipe", None, None),
        P("pipe", "seq", None, None),
        P("pipe", "seq", None, None),
    )
    return jax.shard_map(
        per_device,
        mesh=mesh,
        in_specs=placed,
        out_specs=(
            P("pipe", "seq", None),
            P("pipe", "seq", None, None),
            P("pipe", "seq", None, None),
        ),
        check_vma=False,
    )
```
